32 devices in a mesh: tile: 8 (over y, x, core), depth: 4 (over z).
Axes of the slice: x: 2, y: 2, z: 4, core: 2. Of those that a mesh axis runs over, the one named last changes fastest.
Arguments:
- grid: float32 [4, 32, 32, 1024], P(None, 'tile', 'depth'), may hold values from -6 to 6
- first_moment: float32 [4, 32, 32, 1024], P(None, 'tile', 'depth'), may hold values from -4 to 4
- second_moment: float32 [4, 32, 32, 1024], P(None, 'tile', 'depth'), may hold values from 0.01 to 1
- ray_offset: int32 [32, 1024], P('tile'), may hold values from 0 to 1
- occupancy: int32 [8, 4, 128], P('tile', 'depth'), may hold values 0 or 1
- target: float32 [3, 32, 1024], P(None, 'tile'), may hold values from 0 to 1
Outputs:
- new_grid: float32 [4, 32, 32, 1024], P(None, 'tile', 'depth')
- new_first: float32 [4, 32, 32, 1024], P(None, 'tile', 'depth')
- new_second: float32 [4, 32, 32, 1024], P(None, 'tile', 'depth')
The draws below stay inside these ranges and needn't reach their ends.
All inputs are finite; a program needn't handle non-finite values. No bound on the sum of `occupancy` on one device may be relied on, other than what follows from the above.
Results may differ from the reference program's by a relative error of at most 0.00002.
Values sent between devices are 32-bit elements; how exact they have to be, the bound alone decides.
A program may use at most 64 MiB of HBM per device.

```python
import math
import jax
import jax.numpy as jnp
from jax import lax

CHANNELS = 4
NX = 32
NY = 1024
NZ = 32


def plant(entries, key, smallest, largest):
    longest = entries.shape.index(max(entries.shape))
    spots = []
    for shift in (0, 1):
        where = [jax.random.randint(jax.random.fold_in(key, axis), (), 0, length) for axis, length in enumerate(entries.shape)]
        where[longest] = (where[longest] + shift) % entries.shape[longest]
        spots.append(tuple(where))
    return entries.at[spots[0]].set(smallest).at[spots[1]].set(largest)


def levels(own_key, dims, cuts, least, top_value):
    factor_of, own = 1.0, jax.random.fold_in(own_key, 6)
    for dim, shards_of in cuts:
        steps = jnp.exp(jax.random.uniform(jax.random.fold_in(own, dim), (shards_of,), jnp.float32, least / len(cuts), top_value / len(cuts)))
        factor_of = factor_of * jnp.repeat(steps, dims[dim] // shards_of).reshape([-1 if axis == dim else 1 for axis in range(len(dims))])
    return factor_of


def gaussian(key, extent, deviation, limit, split=(), kind=jnp.bfloat16):
    drawn = deviation * jax.random.normal(key, extent, jnp.float32)
    if split:
        drawn = drawn * levels(key, extent, split, -0.22, 0.18)
    return jnp.clip(drawn, -limit, limit).astype(kind)


def setup_inputs(seed: int = 0) -> dict:
    seeds = jax.random.split(jax.random.key(seed), 7)
    return {
        "grid": gaussian(seeds[0], (CHANNELS, NX, NZ, NY), 1.0, 6.0, ((1, 8), (2, 4)), jnp.float32),
        "first_moment": gaussian(seeds[1], (CHANNELS, NX, NZ, NY), 0.3, 4.0, ((1, 8), (2, 4)), jnp.float32),
        "second_moment": jnp.clip(jnp.exp(math.log(1.0) - 4.6051702 * jax.random.uniform(seeds[2], (CHANNELS, NX, NZ, NY), jnp.float32) ** levels(seeds[2], (CHANNELS, NX, NZ, NY), ((1, 8), (2, 4)), -0.2, 0.2)), 0.01, 1.0),
        "ray_offset": plant(jax.random.randint(seeds[3], (NX, NY), 0, 2), jax.random.fold_in(seeds[3], 1), 0, 1).astype(jnp.int32),
        "occupancy": plant((jax.random.randint(seeds[4], (NX // 4, NZ // 8, NY // 8), 0, 4) < 3).astype(jnp.int32), jax.random.fold_in(seeds[4], 1), 0, 1),
        "target": jnp.clip(1.0 * jax.random.uniform(seeds[5], (3, NX, NY), jnp.float32) ** levels(seeds[5], (3, NX, NY), ((1, 8),), -0.2, 0.2), 0.0, 1.0),
    }


tv_weight = 0.01
beta_one = 0.9
beta_two = 0.95
learn_rate = 0.1
adam_step = 10
epsilon = 1e-08

def total_loss(grid, ray_offset, occ, target):
    planes = grid.shape[2]
    after_rows = jnp.concatenate([grid[:, 1:], jnp.zeros_like(grid[:, :1])], axis=1)
    shares = (ray_offset.astype(jnp.float32) * 0.5)[None, :, None, :]
    features = (1.0 - shares) * grid + shares * after_rows
    sigma = occ * jax.nn.softplus(features[0]) * (4.0 / planes)
    colour = jax.nn.sigmoid(features[1:])
    before = jnp.cumsum(sigma, axis=1) - sigma
    weight = jnp.exp(-before) * -jnp.expm1(-sigma)
    pixel = lax.optimization_barrier(jnp.sum(weight[None] * colour, axis=2)) + jnp.exp(-lax.optimization_barrier(jnp.sum(sigma, axis=1)))[None]
    loss = 0.25 * planes * jnp.sum((pixel - target) ** 2)
    padded = jnp.pad(grid, ((0, 0), (1, 1), (1, 1), (1, 1)))
    smooth = jnp.sum(jnp.diff(padded, axis=1) ** 2) + jnp.sum(jnp.diff(padded, axis=2) ** 2) + jnp.sum(jnp.diff(padded, axis=3) ** 2)
    return loss + tv_weight * smooth

def reference(grid, first_moment, second_moment, ray_offset, occupancy, target):
    occ = occupancy.astype(jnp.float32)
    occ = jnp.repeat(jnp.repeat(jnp.repeat(occ, 4, axis=0), 8, axis=1), 8, axis=2)
    grad = jax.grad(total_loss)(grid, ray_offset, occ, target)
    new_first = beta_one * first_moment + (1.0 - beta_one) * grad
    new_second = beta_two * second_moment + (1.0 - beta_two) * grad * grad
    corr_one = 1.0 - beta_one ** adam_step
    corr_two = 1.0 - beta_two ** adam_step
    new_grid = grid - learn_rate * (new_first / corr_one) / (jnp.sqrt(new_second / corr_two) + epsilon)
    return (new_grid, new_first, new_second)
```

```python
import functools

import jax
import jax.numpy as jnp
from jax import lax
from jax.experimental import pallas as pl
from jax.experimental.pallas import tpu as pltpu
from jax.sharding import PartitionSpec as P

MESH = pl.DeviceIdType.MESH
tv_weight = 0.01
beta_one = 0.9
beta_two = 0.95
learn_rate = 0.1
adam_step = 10
epsilon = 1e-08


def running_sum(x, iota, backward):
    count = x.shape[0]
    step = 1
    while step < count:
        if backward:
            x = x + jnp.where(iota < count - step, pltpu.roll(x, count - step, 0), 0.0)
        else:
            x = x + jnp.where(iota >= step, pltpu.roll(x, step, 0), 0.0)
        step *= 2
    return x


def one_minus_exp(s):
    series = 1.0 / 120 - s * (1.0 / 720)
    for term in (1.0 / 24, 1.0 / 6, 0.5, 1.0):
        series = term - s * series
    return jnp.where(s < 0.25, s * series, 1.0 - jnp.exp(-s))


def sigmoid(x):
    return 1.0 / (1.0 + jnp.exp(-x))


def kernel(
    tiles, depths, pieces,
    grid_h, ray_h, occ_h, tgt_h, grad_ref,
    g, ray, occ_i, tgt, nxt, prv, ext_out, ext_in, zout, zin,
    col, wgt, ntr, dfac,
    seg1_out, seg1_in, seg2_out, seg2_in,
    qd1_out, qd1_in, qd2_out, qd2_in, qdp_in,
    load_sem, halo_send, halo_recv,
    s1_send, s1_recv, s2_send, s2_recv,
    q1_send, q1_recv, q2_send, q2_recv, qp_send, qp_recv,
):
    t, k = lax.axis_index("tile"), lax.axis_index("depth")
    channels, rows, planes, width = g.shape
    last = rows - 1
    piece = width // pieces
    scale = 4.0 / (planes * depths)
    has_prev, has_next = t > 0, t < tiles - 1
    reduces = k < pieces

    loads = [
        pltpu.make_async_copy(src, dst, load_sem.at[i])
        for i, (src, dst) in enumerate(((grid_h, g), (ray_h, ray), (occ_h, occ_i), (tgt_h, tgt)))
    ]
    for load in loads:
        load.start()

    barrier = pltpu.get_barrier_semaphore()
    for d in range(1, depths):
        pl.semaphore_signal(barrier, inc=1, device_id={"depth": lax.rem(k + d, depths)}, device_id_type=MESH)

    @pl.when(has_prev)
    def _():
        for j in range(depths):
            pl.semaphore_signal(barrier, inc=1, device_id={"tile": t - 1, "depth": j}, device_id_type=MESH)

    @pl.when(has_next)
    def _():
        for j in range(depths):
            pl.semaphore_signal(barrier, inc=1, device_id={"tile": t + 1, "depth": j}, device_id_type=MESH)

    @pl.when(jnp.logical_not(has_prev))
    def _():
        prv[...] = jnp.zeros_like(prv)
        ext_in[...] = jnp.zeros_like(ext_in)
        qdp_in[...] = jnp.zeros_like(qdp_in)

    @pl.when(jnp.logical_not(has_next))
    def _():
        nxt[...] = jnp.zeros_like(nxt)

    @pl.when(k == 0)
    def _():
        zin[0] = jnp.zeros(zin.shape[1:], jnp.float32)

    @pl.when(k == depths - 1)
    def _():
        zin[1] = jnp.zeros(zin.shape[1:], jnp.float32)

    for load in loads:
        load.wait()

    blocks = occ_i.shape[2]
    spread = lax.broadcasted_iota(jnp.int32, (blocks, width), 1) // (width // blocks)
    spread = (spread == lax.broadcasted_iota(jnp.int32, (blocks, width), 0)).astype(jnp.float32)
    occ_rows = jnp.broadcast_to(occ_i[0].astype(jnp.float32), (8, blocks))
    occ = jnp.dot(occ_rows, spread, preferred_element_type=jnp.float32)[0:1]
    ext_out[0:1, :] = ray[last : last + 1, :].astype(jnp.float32) * 0.5
    ext_out[1:2, :] = occ
    for c in range(channels):
        for r in range(rows):
            zout[0, c * rows + r : c * rows + r + 1, :] = g[c, r, planes - 1 : planes, :]
            zout[1, c * rows + r : c * rows + r + 1, :] = g[c, r, 0:1, :]

    to_prev = pltpu.make_async_remote_copy(
        g.at[:, 0:1], nxt, halo_send.at[0], halo_recv.at[0], device_id={"tile": t - 1}, device_id_type=MESH
    )
    to_next = pltpu.make_async_remote_copy(
        g.at[:, last:rows], prv, halo_send.at[1], halo_recv.at[1], device_id={"tile": t + 1}, device_id_type=MESH
    )
    ext_next = pltpu.make_async_remote_copy(
        ext_out, ext_in, halo_send.at[2], halo_recv.at[2], device_id={"tile": t + 1}, device_id_type=MESH
    )
    z_back = pltpu.make_async_remote_copy(
        zout.at[0], zin.at[0], halo_send.at[3], halo_recv.at[3], device_id={"depth": k + 1}, device_id_type=MESH
    )
    z_front = pltpu.make_async_remote_copy(
        zout.at[1], zin.at[1], halo_send.at[4], halo_recv.at[4], device_id={"depth": k - 1}, device_id_type=MESH
    )

    partners = depths - 1 + depths * (has_prev.astype(jnp.int32) + has_next.astype(jnp.int32))
    pl.semaphore_wait(barrier, partners)

    @pl.when(has_prev)
    def _():
        to_prev.start()

    @pl.when(has_next)
    def _():
        to_next.start()
        ext_next.start()

    @pl.when(k < depths - 1)
    def _():
        z_back.start()

    @pl.when(k > 0)
    def _():
        z_front.start()

    planes_at = lax.broadcasted_iota(jnp.int32, (planes, width), 0)

    def samples(slot, here, after, share, occ):
        density = here(0) + share * (after(0) - here(0))
        tail = jnp.exp(-jnp.abs(density))
        sigma = occ * (jnp.maximum(density, 0.0) + jnp.log1p(tail)) * scale
        dfac[slot] = occ * scale * jnp.where(density >= 0.0, 1.0, tail) / (1.0 + tail)
        upto = running_sum(sigma, planes_at, False)
        weight = jnp.exp(sigma - upto) * one_minus_exp(sigma)
        after_all = jnp.exp(-upto)
        wgt[slot] = weight
        ntr[slot] = after_all
        out = []
        for c in range(1, channels):
            colour = sigmoid(here(c) + share * (after(c) - here(c)))
            col[slot, c - 1] = colour
            out.append(jnp.sum(weight * colour, axis=0, keepdims=True))
        out.append(after_all[planes - 1 : planes])
        return out

    def share_of(r):
        return ray[r : r + 1, :].astype(jnp.float32) * 0.5

    def put(seg_out, r, values):
        for v in range(channels):
            for p in range(pieces):
                seg_out[p, v, r : r + 1, :] = values[v][:, p * piece : (p + 1) * piece]

    def when_reduces(who, work):
        if pieces < depths:
            pl.when(who < pieces)(work)
        else:
            work()

    def seg_copy(seg_out, seg_in, send, recv, d, source=None):
        to = lax.rem(k + d, depths)
        slot = k if source is None else source
        return pltpu.make_async_remote_copy(
            seg_out.at[to % pieces], seg_in.at[slot], send.at[d], recv.at[slot],
            device_id={"depth": to}, device_id_type=MESH,
        )

    def send_segments(seg_out, seg_in, send, recv):
        for d in range(1, depths):
            when_reduces(lax.rem(k + d, depths), seg_copy(seg_out, seg_in, send, recv, d).start)

        def own():
            seg_in[k] = seg_out[k % pieces]

        when_reduces(k, own)

    def reduce(seg_in, qd_out, send, recv, first, count):
        for d in range(1, depths):
            source = lax.rem(k + d, depths)
            seg_copy(seg_in, seg_in, send, recv, d, source).wait_recv()
        at = pl.ds(pl.multiple_of((k % pieces) * piece, piece), piece)
        fronts = [None]
        front = seg_in[0, 3]
        pixel = [seg_in[0, c] for c in range(3)]
        fronts.append(front)
        for j in range(1, depths):
            for c in range(3):
                pixel[c] = pixel[c] + front * seg_in[j, c]
            front = front * seg_in[j, 3]
            fronts.append(front)
        half = 0.5 * planes * depths
        pg = [half * (pixel[c] + front - tgt[c, first : first + count, at]) for c in range(3)]
        behind = pg[0] + pg[1] + pg[2]
        for j in range(depths - 1, -1, -1):
            for c in range(3):
                qd_out[j, c] = pg[c] if j == 0 else fronts[j] * pg[c]
            qd_out[j, 3] = fronts[j + 1] * behind
            if j:
                behind = pg[0] * seg_in[j, 0] + pg[1] * seg_in[j, 1] + pg[2] * seg_in[j, 2] + seg_in[j, 3] * behind

    def qd_copy(qd_out, qd_in, send, recv, d, source=None):
        to = lax.rem(k + d, depths)
        slot = k % pieces if source is None else source % pieces
        return pltpu.make_async_remote_copy(
            qd_out.at[to], qd_in.at[slot], send.at[d], recv.at[slot],
            device_id={"depth": to}, device_id_type=MESH,
        )

    def qd_copy_next(d, source=None):
        to = lax.rem(k + d, depths)
        slot = k % pieces if source is None else source % pieces
        return pltpu.make_async_remote_copy(
            qd2_out.at[to], qdp_in.at[slot], qp_send.at[d], qp_recv.at[slot],
            device_id={"tile": t + 1, "depth": to}, device_id_type=MESH,
        )

    def send_back(qd_out, qd_in, send, recv):
        for d in range(1, depths):
            qd_copy(qd_out, qd_in, send, recv, d).start()
        qd_in[k % pieces] = qd_out[k]

    def wait_back(qd_in, send, recv):
        for d in range(1, depths):
            source = lax.rem(k + d, depths)
            when_reduces(source, qd_copy(qd_in, qd_in, send, recv, d, source).wait_recv)

    for r in range(last):
        values = samples(r, lambda c: g[c, r], lambda c: g[c, r + 1], share_of(r), occ)
        put(seg1_out, r, values)
    send_segments(seg1_out, seg1_in, s1_send, s1_recv)

    pl.when(has_next)(to_prev.wait_recv)
    values = samples(last, lambda c: g[c, last], lambda c: nxt[c, 0], share_of(last), occ)
    put(seg2_out, 0, values)
    send_segments(seg2_out, seg2_in, s2_send, s2_recv)

    def first_rows():
        reduce(seg1_in, qd1_out, s1_send, s1_recv, 0, last)
        send_back(qd1_out, qd1_in, q1_send, q1_recv)

    when_reduces(k, first_rows)

    def last_row():
        reduce(seg2_in, qd2_out, s2_send, s2_recv, last, 1)
        send_back(qd2_out, qd2_in, q2_send, q2_recv)

        @pl.when(has_next)
        def _():
            for d in range(depths):
                qd_copy_next(d).start()

    when_reduces(k, last_row)

    @pl.when(has_prev)
    def _():
        to_next.wait_recv()
        ext_next.wait_recv()

    samples(rows, lambda c: prv[c, 0], lambda c: g[c, 0], ext_in[0:1, :], ext_in[1:2, :])

    pl.when(k > 0)(z_back.wait_recv)
    pl.when(k < depths - 1)(z_front.wait_recv)
    lanes = lax.broadcasted_iota(jnp.int32, (planes, width), 1)
    for c in range(channels):
        for r in range(rows):
            here = g[c, r]
            i = c * rows + r
            around = (prv[c, 0] if r == 0 else g[c, r - 1]) + (nxt[c, 0] if r == last else g[c, r + 1])
            around += jnp.where(planes_at == 0, zin[0, i : i + 1, :], pltpu.roll(here, 1, 0))
            around += jnp.where(planes_at == planes - 1, zin[1, i : i + 1, :], pltpu.roll(here, planes - 1, 0))
            around += jnp.where(lanes == 0, 0.0, pltpu.roll(here, 1, 1))
            around += jnp.where(lanes == width - 1, 0.0, pltpu.roll(here, width - 1, 1))
            grad_ref[c, r] = 2.0 * tv_weight * (6.0 * here - around)

    def gradient(slot, qd_in, r):
        q = [jnp.concatenate([qd_in[p, v, r : r + 1, :] for p in range(pieces)], axis=1) for v in range(4)]
        u = q[0] * col[slot, 0] + q[1] * col[slot, 1] + q[2] * col[slot, 2]
        weight = wgt[slot]
        part = weight * u
        rest = running_sum(part, planes_at, True) - part
        out = [(ntr[slot] * u - rest - q[3]) * dfac[slot]]
        for c in range(3):
            colour = col[slot, c]
            out.append(q[c] * weight * (colour * (1.0 - colour)))
        return out

    def add(r, factor, values):
        for c in range(channels):
            grad_ref[c, r] += factor * values[c]

    wait_back(qd1_in, q1_send, q1_recv)
    for r in range(last):
        values = gradient(r, qd1_in, r)
        add(r, 1.0 - share_of(r), values)
        add(r + 1, share_of(r), values)
    wait_back(qd2_in, q2_send, q2_recv)
    add(last, 1.0 - share_of(last), gradient(last, qd2_in, 0))

    @pl.when(has_prev)
    def _():
        for d in range(depths):
            source = lax.rem(k + d, depths)
            when_reduces(source, qd_copy_next(d, source).wait_recv)

    add(0, ext_in[0:1, :], gradient(rows, qdp_in, 0))

    pl.when(has_prev)(to_prev.wait_send)

    @pl.when(has_next)
    def _():
        to_next.wait_send()
        ext_next.wait_send()

    pl.when(k < depths - 1)(z_back.wait_send)
    pl.when(k > 0)(z_front.wait_send)
    for d in range(1, depths):
        to = lax.rem(k + d, depths)
        when_reduces(to, seg_copy(seg1_out, seg1_in, s1_send, s1_recv, d).wait_send)
        when_reduces(to, seg_copy(seg2_out, seg2_in, s2_send, s2_recv, d).wait_send)

    def sent_back():
        for d in range(1, depths):
            qd_copy(qd1_out, qd1_in, q1_send, q1_recv, d).wait_send()
            qd_copy(qd2_out, qd2_in, q2_send, q2_recv, d).wait_send()

        @pl.when(has_next)
        def _():
            for d in range(depths):
                qd_copy_next(d).wait_send()

    when_reduces(k, sent_back)


def gradient_of_loss(grid, ray_offset, occupancy, target, tiles, depths):
    channels, rows, planes, width = grid.shape
    pieces = max(1, min(depths, width // 128))
    piece = width // pieces
    f32 = jnp.float32
    vmem, dma = pltpu.VMEM, pltpu.SemaphoreType.DMA
    scratch = [
        vmem(grid.shape, f32), vmem(ray_offset.shape, jnp.int32), vmem(occupancy.shape, jnp.int32),
        vmem(target.shape, f32),
        vmem((channels, 1, planes, width), f32), vmem((channels, 1, planes, width), f32),
        vmem((8, width), f32), vmem((8, width), f32),
        vmem((2, channels * rows, width), f32), vmem((2, channels * rows, width), f32),
        vmem((rows + 1, 3, planes, width), f32), vmem((rows + 1, planes, width), f32),
        vmem((rows + 1, planes, width), f32), vmem((rows + 1, planes, width), f32),
    ]
    for count in (rows - 1, 1):
        scratch += [vmem((pieces, 4, count, piece), f32), vmem((depths, 4, count, piece), f32)]
    for count in (rows - 1, 1):
        scratch += [vmem((depths, 4, count, piece), f32), vmem((pieces, 4, count, piece), f32)]
    scratch += [vmem((pieces, 4, 1, piece), f32)]
    scratch += [dma((4,)), dma((5,)), dma((5,))] + [dma((depths,))] * 10
    hbm = pl.BlockSpec(memory_space=pl.ANY)
    return pl.pallas_call(
        functools.partial(kernel, tiles, depths, pieces),
        out_shape=jax.ShapeDtypeStruct(grid.shape, f32),
        in_specs=[hbm] * 4,
        out_specs=pl.BlockSpec(memory_space=pltpu.VMEM),
        scratch_shapes=scratch,
        compiler_params=pltpu.CompilerParams(
            collective_id=0, has_side_effects=True, vmem_limit_bytes=24 * 2**20
        ),
        cost_estimate=pl.CostEstimate(flops=10**7, bytes_accessed=2**20, transcendentals=10**6),
    )(grid, ray_offset, occupancy, target)


def solution(mesh):
    tiles, depths = mesh.shape["tile"], mesh.shape["depth"]
    voxels = P(None, "tile", "depth", None)
    in_specs = (voxels, voxels, voxels, P("tile", None), P("tile", "depth", None), P(None, "tile", None))

    def body(grid, first_moment, second_moment, ray_offset, occupancy, target):
        grad = gradient_of_loss(grid, ray_offset, occupancy, target, tiles, depths)
        new_first = beta_one * first_moment + (1.0 - beta_one) * grad
        new_second = beta_two * second_moment + (1.0 - beta_two) * grad * grad
        corr_one = 1.0 - beta_one**adam_step
        corr_two = 1.0 - beta_two**adam_step
        new_grid = grid - learn_rate * (new_first / corr_one) / (jnp.sqrt(new_second / corr_two) + epsilon)
        return (new_grid, new_first, new_second)

    return jax.shard_map(body, mesh=mesh, in_specs=in_specs, out_specs=(voxels,) * 3, check_vma=False)
```

```python
import functools

import jax
import jax.numpy as jnp
from jax import lax
from jax.experimental import pallas as pl
from jax.experimental.pallas import tpu as pltpu
from jax.sharding import PartitionSpec as P

MESH = pl.DeviceIdType.MESH
tv_weight = 0.01
beta_one = 0.9
beta_two = 0.95
learn_rate = 0.1
adam_step = 10
epsilon = 1e-08


def running_sum(x, iota, backward):
    count = x.shape[0]
    step = 1
    while step < count:
        if backward:
            x = x + jnp.where(iota < count - step, pltpu.roll(x, count - step, 0), 0.0)
        else:
            x = x + jnp.where(iota >= step, pltpu.roll(x, step, 0), 0.0)
        step *= 2
    return x


def one_minus_exp(s):
    series = 1.0 / 120 - s * (1.0 / 720)
    for term in (1.0 / 24, 1.0 / 6, 0.5, 1.0):
        series = term - s * series
    return jnp.where(s < 0.25, s * series, 1.0 - jnp.exp(-s))


def sigmoid(x):
    return 1.0 / (1.0 + jnp.exp(-x))


def kernel(
    tiles, depths, pieces,
    grid_h, ray_h, occ_h, tgt_h, grad_ref,
    g, ray, occ_i, tgt, nxt, prv, ext_out, ext_in, zout, zin,
    col, wgt, ntr, dfac,
    seg1_out, seg1_in, seg2_out, seg2_in,
    qd1_out, qd1_in, qd2_out, qd2_in, qdp_in,
    load_sem, halo_send, halo_recv,
    s1_send, s1_recv, s2_send, s2_recv,
    q1_send, q1_recv, q2_send, q2_recv, qp_send, qp_recv,
):
    t, k = lax.axis_index("tile"), lax.axis_index("depth")
    channels, rows, planes, width = g.shape
    last = rows - 1
    piece = width // pieces
    scale = 4.0 / (planes * depths)
    has_prev, has_next = t > 0, t < tiles - 1
    reduces = k < pieces

    loads = [
        pltpu.make_async_copy(src, dst, load_sem.at[i])
        for i, (src, dst) in enumerate(((grid_h, g), (ray_h, ray), (occ_h, occ_i), (tgt_h, tgt)))
    ]
    for load in loads:
        load.start()

    barrier = pltpu.get_barrier_semaphore()
    for d in range(1, depths):
        pl.semaphore_signal(barrier, inc=1, device_id={"depth": lax.rem(k + d, depths)}, device_id_type=MESH)

    @pl.when(has_prev)
    def _():
        for j in range(depths):
            pl.semaphore_signal(barrier, inc=1, device_id={"tile": t - 1, "depth": j}, device_id_type=MESH)

    @pl.when(has_next)
    def _():
        for j in range(depths):
            pl.semaphore_signal(barrier, inc=1, device_id={"tile": t + 1, "depth": j}, device_id_type=MESH)

    @pl.when(jnp.logical_not(has_prev))
    def _():
        prv[...] = jnp.zeros_like(prv)
        ext_in[...] = jnp.zeros_like(ext_in)
        qdp_in[...] = jnp.zeros_like(qdp_in)

    @pl.when(jnp.logical_not(has_next))
    def _():
        nxt[...] = jnp.zeros_like(nxt)

    @pl.when(k == 0)
    def _():
        zin[0] = jnp.zeros(zin.shape[1:], jnp.float32)

    @pl.when(k == depths - 1)
    def _():
        zin[1] = jnp.zeros(zin.shape[1:], jnp.float32)

    for load in loads:
        load.wait()

    blocks = occ_i.shape[2]
    spread = lax.broadcasted_iota(jnp.int32, (blocks, width), 1) // (width // blocks)
    spread = (spread == lax.broadcasted_iota(jnp.int32, (blocks, width), 0)).astype(jnp.float32)
    occ_rows = jnp.broadcast_to(occ_i[0].astype(jnp.float32), (8, blocks))
    occ = jnp.dot(occ_rows, spread, preferred_element_type=jnp.float32)[0:1]
    ext_out[0:1, :] = ray[last : last + 1, :].astype(jnp.float32) * 0.5
    ext_out[1:2, :] = occ
    for c in range(channels):
        for r in range(rows):
            zout[0, c * rows + r : c * rows + r + 1, :] = g[c, r, planes - 1 : planes, :]
            zout[1, c * rows + r : c * rows + r + 1, :] = g[c, r, 0:1, :]

    to_prev = pltpu.make_async_remote_copy(
        g.at[:, 0:1], nxt, halo_send.at[0], halo_recv.at[0], device_id={"tile": t - 1}, device_id_type=MESH
    )
    to_next = pltpu.make_async_remote_copy(
        g.at[:, last:rows], prv, halo_send.at[1], halo_recv.at[1], device_id={"tile": t + 1}, device_id_type=MESH
    )
    ext_next = pltpu.make_async_remote_copy(
        ext_out, ext_in, halo_send.at[2], halo_recv.at[2], device_id={"tile": t + 1}, device_id_type=MESH
    )
    z_back = pltpu.make_async_remote_copy(
        zout.at[0], zin.at[0], halo_send.at[3], halo_recv.at[3], device_id={"depth": k + 1}, device_id_type=MESH
    )
    z_front = pltpu.make_async_remote_copy(
        zout.at[1], zin.at[1], halo_send.at[4], halo_recv.at[4], device_id={"depth": k - 1}, device_id_type=MESH
    )

    partners = depths - 1 + depths * (has_prev.astype(jnp.int32) + has_next.astype(jnp.int32))
    pl.semaphore_wait(barrier, partners)

    @pl.when(has_prev)
    def _():
        to_prev.start()

    @pl.when(k < depths - 1)
    def _():
        z_back.start()

    @pl.when(k > 0)
    def _():
        z_front.start()

    planes_at = lax.broadcasted_iota(jnp.int32, (planes, width), 0)

    def samples(slot, here, after, share, occ):
        density = here(0) + share * (after(0) - here(0))
        tail = jnp.exp(-jnp.abs(density))
        sigma = occ * (jnp.maximum(density, 0.0) + jnp.log1p(tail)) * scale
        dfac[slot] = occ * scale * jnp.where(density >= 0.0, 1.0, tail) / (1.0 + tail)
        upto = running_sum(sigma, planes_at, False)
        weight = jnp.exp(sigma - upto) * one_minus_exp(sigma)
        after_all = jnp.exp(-upto)
        wgt[slot] = weight
        ntr[slot] = after_all
        out = []
        for c in range(1, channels):
            colour = sigmoid(here(c) + share * (after(c) - here(c)))
            col[slot, c - 1] = colour
            out.append(jnp.sum(weight * colour, axis=0, keepdims=True))
        out.append(after_all[planes - 1 : planes])
        return out

    def share_of(r):
        return ray[r : r + 1, :].astype(jnp.float32) * 0.5

    def put(seg_out, r, values):
        for v in range(channels):
            for p in range(pieces):
                seg_out[p, v, r : r + 1, :] = values[v][:, p * piece : (p + 1) * piece]

    def when_reduces(who, work):
        if pieces < depths:
            pl.when(who < pieces)(work)
        else:
            work()

    def seg_copy(seg_out, seg_in, send, recv, d, source=None):
        to = lax.rem(k + d, depths)
        slot = k if source is None else source
        return pltpu.make_async_remote_copy(
            seg_out.at[to % pieces], seg_in.at[slot], send.at[d], recv.at[slot],
            device_id={"depth": to}, device_id_type=MESH,
        )

    def send_segments(seg_out, seg_in, send, recv):
        for d in range(1, depths):
            when_reduces(lax.rem(k + d, depths), seg_copy(seg_out, seg_in, send, recv, d).start)

        def own():
            seg_in[k] = seg_out[k % pieces]

        when_reduces(k, own)

    def reduce(seg_in, qd_out, send, recv, first, count):
        for d in range(1, depths):
            source = lax.rem(k + d, depths)
            seg_copy(seg_in, seg_in, send, recv, d, source).wait_recv()
        at = pl.ds(pl.multiple_of((k % pieces) * piece, piece), piece)
        fronts = [None]
        front = seg_in[0, 3]
        pixel = [seg_in[0, c] for c in range(3)]
        fronts.append(front)
        for j in range(1, depths):
            for c in range(3):
                pixel[c] = pixel[c] + front * seg_in[j, c]
            front = front * seg_in[j, 3]
            fronts.append(front)
        half = 0.5 * planes * depths
        pg = [half * (pixel[c] + front - tgt[c, first : first + count, at]) for c in range(3)]
        behind = pg[0] + pg[1] + pg[2]
        for j in range(depths - 1, -1, -1):
            for c in range(3):
                qd_out[j, c] = pg[c] if j == 0 else fronts[j] * pg[c]
            qd_out[j, 3] = fronts[j + 1] * behind
            if j:
                behind = pg[0] * seg_in[j, 0] + pg[1] * seg_in[j, 1] + pg[2] * seg_in[j, 2] + seg_in[j, 3] * behind

    def qd_copy(qd_out, qd_in, send, recv, d, source=None):
        to = lax.rem(k + d, depths)
        slot = k % pieces if source is None else source % pieces
        return pltpu.make_async_remote_copy(
            qd_out.at[to], qd_in.at[slot], send.at[d], recv.at[slot],
            device_id={"depth": to}, device_id_type=MESH,
        )

    def qd_copy_next(d, source=None):
        to = lax.rem(k + d, depths)
        slot = k % pieces if source is None else source % pieces
        return pltpu.make_async_remote_copy(
            qd2_out.at[to], qdp_in.at[slot], qp_send.at[d], qp_recv.at[slot],
            device_id={"tile": t + 1, "depth": to}, device_id_type=MESH,
        )

    def send_back(qd_out, qd_in, send, recv):
        for d in range(1, depths):
            qd_copy(qd_out, qd_in, send, recv, d).start()
        qd_in[k % pieces] = qd_out[k]

    def wait_back(qd_in, send, recv):
        for d in range(1, depths):
            source = lax.rem(k + d, depths)
            when_reduces(source, qd_copy(qd_in, qd_in, send, recv, d, source).wait_recv)

    for r in range(last):
        values = samples(r, lambda c: g[c, r], lambda c: g[c, r + 1], share_of(r), occ)
        put(seg1_out, r, values)
    send_segments(seg1_out, seg1_in, s1_send, s1_recv)

    @pl.when(has_next)
    def _():
        to_next.start()
        ext_next.start()

    lanes = lax.broadcasted_iota(jnp.int32, (planes, width), 1)
    for c in range(channels):
        for r in range(rows):
            here = g[c, r]
            around = jnp.where(planes_at == 0, 0.0, pltpu.roll(here, 1, 0))
            around += jnp.where(planes_at == planes - 1, 0.0, pltpu.roll(here, planes - 1, 0))
            around += jnp.where(lanes == 0, 0.0, pltpu.roll(here, 1, 1))
            around += jnp.where(lanes == width - 1, 0.0, pltpu.roll(here, width - 1, 1))
            if r > 0:
                around += g[c, r - 1]
            if r < last:
                around += g[c, r + 1]
            grad_ref[c, r] = 2.0 * tv_weight * (6.0 * here - around)

    pl.when(has_next)(to_prev.wait_recv)
    values = samples(last, lambda c: g[c, last], lambda c: nxt[c, 0], share_of(last), occ)
    put(seg2_out, 0, values)
    send_segments(seg2_out, seg2_in, s2_send, s2_recv)

    def first_rows():
        reduce(seg1_in, qd1_out, s1_send, s1_recv, 0, last)
        send_back(qd1_out, qd1_in, q1_send, q1_recv)

    when_reduces(k, first_rows)

    @pl.when(has_prev)
    def _():
        to_next.wait_recv()
        ext_next.wait_recv()

    samples(rows, lambda c: prv[c, 0], lambda c: g[c, 0], ext_in[0:1, :], ext_in[1:2, :])

    def last_row():
        reduce(seg2_in, qd2_out, s2_send, s2_recv, last, 1)
        send_back(qd2_out, qd2_in, q2_send, q2_recv)

        @pl.when(has_next)
        def _():
            for d in range(depths):
                qd_copy_next(d).start()

    when_reduces(k, last_row)

    pl.when(k > 0)(z_back.wait_recv)
    pl.when(k < depths - 1)(z_front.wait_recv)
    for c in range(channels):
        for r in range(rows):
            i = c * rows + r
            grad_ref[c, r, 0:1, :] -= 2.0 * tv_weight * zin[0, i : i + 1, :]
            grad_ref[c, r, planes - 1 : planes, :] -= 2.0 * tv_weight * zin[1, i : i + 1, :]
        grad_ref[c, 0] -= 2.0 * tv_weight * prv[c, 0]
        grad_ref[c, last] -= 2.0 * tv_weight * nxt[c, 0]

    def gradient(slot, qd_in, r):
        q = [jnp.concatenate([qd_in[p, v, r : r + 1, :] for p in range(pieces)], axis=1) for v in range(4)]
        u = q[0] * col[slot, 0] + q[1] * col[slot, 1] + q[2] * col[slot, 2]
        weight = wgt[slot]
        part = weight * u
        rest = running_sum(part, planes_at, True) - part
        out = [(ntr[slot] * u - rest - q[3]) * dfac[slot]]
        for c in range(3):
            colour = col[slot, c]
            out.append(q[c] * weight * (colour * (1.0 - colour)))
        return out

    def add(r, factor, values):
        for c in range(channels):
            grad_ref[c, r] += factor * values[c]

    wait_back(qd1_in, q1_send, q1_recv)
    for r in range(last):
        values = gradient(r, qd1_in, r)
        add(r, 1.0 - share_of(r), values)
        add(r + 1, share_of(r), values)
    wait_back(qd2_in, q2_send, q2_recv)
    add(last, 1.0 - share_of(last), gradient(last, qd2_in, 0))

    @pl.when(has_prev)
    def _():
        for d in range(depths):
            source = lax.rem(k + d, depths)
            when_reduces(source, qd_copy_next(d, source).wait_recv)

    add(0, ext_in[0:1, :], gradient(rows, qdp_in, 0))

    pl.when(has_prev)(to_prev.wait_send)

    @pl.when(has_next)
    def _():
        to_next.wait_send()
        ext_next.wait_send()

    pl.when(k < depths - 1)(z_back.wait_send)
    pl.when(k > 0)(z_front.wait_send)
    for d in range(1, depths):
        to = lax.rem(k + d, depths)
        when_reduces(to, seg_copy(seg1_out, seg1_in, s1_send, s1_recv, d).wait_send)
        when_reduces(to, seg_copy(seg2_out, seg2_in, s2_send, s2_recv, d).wait_send)

    def sent_back():
        for d in range(1, depths):
            qd_copy(qd1_out, qd1_in, q1_send, q1_recv, d).wait_send()
            qd_copy(qd2_out, qd2_in, q2_send, q2_recv, d).wait_send()

        @pl.when(has_next)
        def _():
            for d in range(depths):
                qd_copy_next(d).wait_send()

    when_reduces(k, sent_back)


def gradient_of_loss(grid, ray_offset, occupancy, target, tiles, depths):
    channels, rows, planes, width = grid.shape
    pieces = max(1, min(depths, width // 128))
    piece = width // pieces
    f32 = jnp.float32
    vmem, dma = pltpu.VMEM, pltpu.SemaphoreType.DMA
    scratch = [
        vmem(grid.shape, f32), vmem(ray_offset.shape, jnp.int32), vmem(occupancy.shape, jnp.int32),
        vmem(target.shape, f32),
        vmem((channels, 1, planes, width), f32), vmem((channels, 1, planes, width), f32),
        vmem((8, width), f32), vmem((8, width), f32),
        vmem((2, channels * rows, width), f32), vmem((2, channels * rows, width), f32),
        vmem((rows + 1, 3, planes, width), f32), vmem((rows + 1, planes, width), f32),
        vmem((rows + 1, planes, width), f32), vmem((rows + 1, planes, width), f32),
    ]
    for count in (rows - 1, 1):
        scratch += [vmem((pieces, 4, count, piece), f32), vmem((depths, 4, count, piece), f32)]
    for count in (rows - 1, 1):
        scratch += [vmem((depths, 4, count, piece), f32), vmem((pieces, 4, count, piece), f32)]
    scratch += [vmem((pieces, 4, 1, piece), f32)]
    scratch += [dma((4,)), dma((5,)), dma((5,))] + [dma((depths,))] * 10
    hbm = pl.BlockSpec(memory_space=pltpu.HBM)
    return pl.pallas_call(
        functools.partial(kernel, tiles, depths, pieces),
        out_shape=jax.ShapeDtypeStruct(grid.shape, f32),
        in_specs=[hbm] * 4,
        out_specs=pl.BlockSpec(memory_space=pltpu.VMEM),
        scratch_shapes=scratch,
        compiler_params=pltpu.CompilerParams(
            collective_id=0, has_side_effects=True, vmem_limit_bytes=60 * 2**20
        ),
        cost_estimate=pl.CostEstimate(flops=10**7, bytes_accessed=2**20, transcendentals=10**6),
    )(grid, ray_offset, occupancy, target)


def solution(mesh):
    tiles, depths = mesh.shape["tile"], mesh.shape["depth"]
    voxels = P(None, "tile", "depth", None)
    in_specs = (voxels, voxels, voxels, P("tile", None), P("tile", "depth", None), P(None, "tile", None))

    def body(grid, first_moment, second_moment, ray_offset, occupancy, target):
        grad = gradient_of_loss(grid, ray_offset, occupancy, target, tiles, depths)
        new_first = beta_one * first_moment + (1.0 - beta_one) * grad
        new_second = beta_two * second_moment + (1.0 - beta_two) * grad * grad
        corr_one = 1.0 - beta_one**adam_step
        corr_two = 1.0 - beta_two**adam_step
        new_grid = grid - learn_rate * (new_first / corr_one) / (jnp.sqrt(new_second / corr_two) + epsilon)
        return (new_grid, new_first, new_second)

    return jax.shard_map(body, mesh=mesh, in_specs=in_specs, out_specs=(voxels,) * 3, check_vma=False)
```

```python
import functools

import jax
import jax.numpy as jnp
from jax import lax
from jax.experimental import pallas as pl
from jax.experimental.pallas import tpu as pltpu
from jax.sharding import PartitionSpec as P

MESH = pl.DeviceIdType.MESH
tv_weight = 0.01
beta_one = 0.9
beta_two = 0.95
learn_rate = 0.1
adam_step = 10
epsilon = 1e-08


def running_sum(x, iota, backward):
    count = x.shape[0]
    step = 1
    while step < count:
        if backward:
            x = x + jnp.where(iota < count - step, pltpu.roll(x, count - step, 0), 0.0)
        else:
            x = x + jnp.where(iota >= step, pltpu.roll(x, step, 0), 0.0)
        step *= 2
    return x


def one_minus_exp(s):
    series = 1.0 / 120 - s * (1.0 / 720)
    for term in (1.0 / 24, 1.0 / 6, 0.5, 1.0):
        series = term - s * series
    return jnp.where(s < 0.25, s * series, 1.0 - jnp.exp(-s))


def sigmoid(x):
    return 1.0 / (1.0 + jnp.exp(-x))


def kernel(
    tiles, depths, pieces,
    grid_h, ray_h, occ_h, tgt_h, grad_ref,
    g, ray, occ_i, tgt, nxt, prv, ext_out, ext_in, zout, zin,
    col, wgt, ntr, dfac,
    seg1_out, seg1_in, seg2_out, seg2_in,
    qd1_out, qd1_in, qd2_out, qd2_in, qdp_in,
    load_sem, halo_send, halo_recv,
    s1_send, s1_recv, s2_send, s2_recv,
    q1_send, q1_recv, q2_send, q2_recv, qp_send, qp_recv,
):
    t, k = lax.axis_index("tile"), lax.axis_index("depth")
    channels, rows, planes, width = g.shape
    last = rows - 1
    piece = width // pieces
    scale = 4.0 / (planes * depths)
    has_prev, has_next = t > 0, t < tiles - 1
    reduces = k < pieces

    loads = [
        pltpu.make_async_copy(src, dst, load_sem.at[i])
        for i, (src, dst) in enumerate(((grid_h, g), (ray_h, ray), (occ_h, occ_i), (tgt_h, tgt)))
    ]
    for load in loads:
        load.start()

    barrier = pltpu.get_barrier_semaphore()
    for d in range(1, depths):
        pl.semaphore_signal(barrier, inc=1, device_id={"depth": lax.rem(k + d, depths)}, device_id_type=MESH)

    @pl.when(has_prev)
    def _():
        for j in range(depths):
            pl.semaphore_signal(barrier, inc=1, device_id={"tile": t - 1, "depth": j}, device_id_type=MESH)

    @pl.when(has_next)
    def _():
        for j in range(depths):
            pl.semaphore_signal(barrier, inc=1, device_id={"tile": t + 1, "depth": j}, device_id_type=MESH)

    @pl.when(jnp.logical_not(has_prev))
    def _():
        prv[...] = jnp.zeros_like(prv)
        ext_in[...] = jnp.zeros_like(ext_in)
        qdp_in[...] = jnp.zeros_like(qdp_in)

    @pl.when(jnp.logical_not(has_next))
    def _():
        nxt[...] = jnp.zeros_like(nxt)

    @pl.when(k == 0)
    def _():
        zin[0] = jnp.zeros(zin.shape[1:], jnp.float32)

    @pl.when(k == depths - 1)
    def _():
        zin[1] = jnp.zeros(zin.shape[1:], jnp.float32)

    to_prev = pltpu.make_async_remote_copy(
        grid_h.at[:, 0:1], nxt, halo_send.at[0], halo_recv.at[0], device_id={"tile": t - 1}, device_id_type=MESH
    )
    to_next = pltpu.make_async_remote_copy(
        g.at[:, last:rows], prv, halo_send.at[1], halo_recv.at[1], device_id={"tile": t + 1}, device_id_type=MESH
    )
    ext_next = pltpu.make_async_remote_copy(
        ext_out, ext_in, halo_send.at[2], halo_recv.at[2], device_id={"tile": t + 1}, device_id_type=MESH
    )
    z_back = pltpu.make_async_remote_copy(
        zout.at[0], zin.at[0], halo_send.at[3], halo_recv.at[3], device_id={"depth": k + 1}, device_id_type=MESH
    )
    z_front = pltpu.make_async_remote_copy(
        zout.at[1], zin.at[1], halo_send.at[4], halo_recv.at[4], device_id={"depth": k - 1}, device_id_type=MESH
    )

    partners = depths - 1 + depths * (has_prev.astype(jnp.int32) + has_next.astype(jnp.int32))
    pl.semaphore_wait(barrier, partners)

    @pl.when(has_prev)
    def _():
        to_prev.start()

    for load in loads:
        load.wait()

    blocks = occ_i.shape[2]
    spread = lax.broadcasted_iota(jnp.int32, (blocks, width), 1) // (width // blocks)
    spread = (spread == lax.broadcasted_iota(jnp.int32, (blocks, width), 0)).astype(jnp.float32)
    occ_rows = jnp.broadcast_to(occ_i[0].astype(jnp.float32), (8, blocks))
    occ = jnp.dot(occ_rows, spread, preferred_element_type=jnp.float32)[0:1]
    ext_out[0:1, :] = ray[last : last + 1, :].astype(jnp.float32) * 0.5
    ext_out[1:2, :] = occ
    for c in range(channels):
        for r in range(rows):
            zout[0, c * rows + r : c * rows + r + 1, :] = g[c, r, planes - 1 : planes, :]
            zout[1, c * rows + r : c * rows + r + 1, :] = g[c, r, 0:1, :]

    @pl.when(k < depths - 1)
    def _():
        z_back.start()

    @pl.when(k > 0)
    def _():
        z_front.start()

    planes_at = lax.broadcasted_iota(jnp.int32, (planes, width), 0)

    def samples(slot, here, after, share, occ):
        density = here(0) + share * (after(0) - here(0))
        tail = jnp.exp(-jnp.abs(density))
        sigma = occ * (jnp.maximum(density, 0.0) + jnp.log1p(tail)) * scale
        dfac[slot] = occ * scale * jnp.where(density >= 0.0, 1.0, tail) / (1.0 + tail)
        upto = running_sum(sigma, planes_at, False)
        weight = jnp.exp(sigma - upto) * one_minus_exp(sigma)
        after_all = jnp.exp(-upto)
        wgt[slot] = weight
        ntr[slot] = after_all
        out = []
        for c in range(1, channels):
            colour = sigmoid(here(c) + share * (after(c) - here(c)))
            col[slot, c - 1] = colour
            out.append(jnp.sum(weight * colour, axis=0, keepdims=True))
        out.append(after_all[planes - 1 : planes])
        return out

    def share_of(r):
        return ray[r : r + 1, :].astype(jnp.float32) * 0.5

    def put(seg_out, r, values):
        for v in range(channels):
            for p in range(pieces):
                seg_out[p, v, r : r + 1, :] = values[v][:, p * piece : (p + 1) * piece]

    def when_reduces(who, work):
        if pieces < depths:
            pl.when(who < pieces)(work)
        else:
            work()

    def seg_copy(seg_out, seg_in, send, recv, d, source=None):
        to = lax.rem(k + d, depths)
        slot = k if source is None else source
        return pltpu.make_async_remote_copy(
            seg_out.at[to % pieces], seg_in.at[slot], send.at[d], recv.at[slot],
            device_id={"depth": to}, device_id_type=MESH,
        )

    def send_segments(seg_out, seg_in, send, recv):
        for d in range(1, depths):
            when_reduces(lax.rem(k + d, depths), seg_copy(seg_out, seg_in, send, recv, d).start)

        def own():
            seg_in[k] = seg_out[k % pieces]

        when_reduces(k, own)

    def reduce(seg_in, qd_out, send, recv, first, count):
        for d in range(1, depths):
            source = lax.rem(k + d, depths)
            seg_copy(seg_in, seg_in, send, recv, d, source).wait_recv()
        at = pl.ds(pl.multiple_of((k % pieces) * piece, piece), piece)
        fronts = [None]
        front = seg_in[0, 3]
        pixel = [seg_in[0, c] for c in range(3)]
        fronts.append(front)
        for j in range(1, depths):
            for c in range(3):
                pixel[c] = pixel[c] + front * seg_in[j, c]
            front = front * seg_in[j, 3]
            fronts.append(front)
        half = 0.5 * planes * depths
        pg = [half * (pixel[c] + front - tgt[c, first : first + count, at]) for c in range(3)]
        behind = pg[0] + pg[1] + pg[2]
        for j in range(depths - 1, -1, -1):
            for c in range(3):
                qd_out[j, c] = pg[c] if j == 0 else fronts[j] * pg[c]
            qd_out[j, 3] = fronts[j + 1] * behind
            if j:
                behind = pg[0] * seg_in[j, 0] + pg[1] * seg_in[j, 1] + pg[2] * seg_in[j, 2] + seg_in[j, 3] * behind

    def qd_copy(qd_out, qd_in, send, recv, d, source=None):
        to = lax.rem(k + d, depths)
        slot = k % pieces if source is None else source % pieces
        return pltpu.make_async_remote_copy(
            qd_out.at[to], qd_in.at[slot], send.at[d], recv.at[slot],
            device_id={"depth": to}, device_id_type=MESH,
        )

    def qd_copy_next(d, source=None):
        to = lax.rem(k + d, depths)
        slot = k % pieces if source is None else source % pieces
        return pltpu.make_async_remote_copy(
            qd2_out.at[to], qdp_in.at[slot], qp_send.at[d], qp_recv.at[slot],
            device_id={"tile": t + 1, "depth": to}, device_id_type=MESH,
        )

    def send_back(qd_out, qd_in, send, recv):
        for d in range(1, depths):
            qd_copy(qd_out, qd_in, send, recv, d).start()
        qd_in[k % pieces] = qd_out[k]

    def wait_back(qd_in, send, recv):
        for d in range(1, depths):
            source = lax.rem(k + d, depths)
            when_reduces(source, qd_copy(qd_in, qd_in, send, recv, d, source).wait_recv)

    for r in range(last):
        values = samples(r, lambda c: g[c, r], lambda c: g[c, r + 1], share_of(r), occ)
        put(seg1_out, r, values)
    send_segments(seg1_out, seg1_in, s1_send, s1_recv)

    @pl.when(has_next)
    def _():
        to_next.start()
        ext_next.start()

    lanes = lax.broadcasted_iota(jnp.int32, (planes, width), 1)
    for c in range(channels):
        for r in range(rows):
            here = g[c, r]
            around = jnp.where(planes_at == 0, 0.0, pltpu.roll(here, 1, 0))
            around += jnp.where(planes_at == planes - 1, 0.0, pltpu.roll(here, planes - 1, 0))
            around += jnp.where(lanes == 0, 0.0, pltpu.roll(here, 1, 1))
            around += jnp.where(lanes == width - 1, 0.0, pltpu.roll(here, width - 1, 1))
            if r > 0:
                around += g[c, r - 1]
            if r < last:
                around += g[c, r + 1]
            grad_ref[c, r] = 2.0 * tv_weight * (6.0 * here - around)

    pl.when(has_next)(to_prev.wait_recv)
    values = samples(last, lambda c: g[c, last], lambda c: nxt[c, 0], share_of(last), occ)
    put(seg2_out, 0, values)
    send_segments(seg2_out, seg2_in, s2_send, s2_recv)

    def first_rows():
        reduce(seg1_in, qd1_out, s1_send, s1_recv, 0, last)
        send_back(qd1_out, qd1_in, q1_send, q1_recv)

    when_reduces(k, first_rows)

    @pl.when(has_prev)
    def _():
        to_next.wait_recv()
        ext_next.wait_recv()

    samples(rows, lambda c: prv[c, 0], lambda c: g[c, 0], ext_in[0:1, :], ext_in[1:2, :])

    def last_row():
        reduce(seg2_in, qd2_out, s2_send, s2_recv, last, 1)
        send_back(qd2_out, qd2_in, q2_send, q2_recv)

        @pl.when(has_next)
        def _():
            for d in range(depths):
                qd_copy_next(d).start()

    when_reduces(k, last_row)

    pl.when(k > 0)(z_back.wait_recv)
    pl.when(k < depths - 1)(z_front.wait_recv)
    for c in range(channels):
        for r in range(rows):
            i = c * rows + r
            grad_ref[c, r, 0:1, :] -= 2.0 * tv_weight * zin[0, i : i + 1, :]
            grad_ref[c, r, planes - 1 : planes, :] -= 2.0 * tv_weight * zin[1, i : i + 1, :]
        grad_ref[c, 0] -= 2.0 * tv_weight * prv[c, 0]
        grad_ref[c, last] -= 2.0 * tv_weight * nxt[c, 0]

    def gradient(slot, qd_in, r):
        q = [jnp.concatenate([qd_in[p, v, r : r + 1, :] for p in range(pieces)], axis=1) for v in range(4)]
        u = q[0] * col[slot, 0] + q[1] * col[slot, 1] + q[2] * col[slot, 2]
        weight = wgt[slot]
        part = weight * u
        rest = running_sum(part, planes_at, True) - part
        out = [(ntr[slot] * u - rest - q[3]) * dfac[slot]]
        for c in range(3):
            colour = col[slot, c]
            out.append(q[c] * weight * (colour * (1.0 - colour)))
        return out

    def add(r, factor, values):
        for c in range(channels):
            grad_ref[c, r] += factor * values[c]

    wait_back(qd1_in, q1_send, q1_recv)
    for r in range(last):
        values = gradient(r, qd1_in, r)
        add(r, 1.0 - share_of(r), values)
        add(r + 1, share_of(r), values)
    wait_back(qd2_in, q2_send, q2_recv)
    add(last, 1.0 - share_of(last), gradient(last, qd2_in, 0))

    @pl.when(has_prev)
    def _():
        for d in range(depths):
            source = lax.rem(k + d, depths)
            when_reduces(source, qd_copy_next(d, source).wait_recv)

    add(0, ext_in[0:1, :], gradient(rows, qdp_in, 0))

    pl.when(has_prev)(to_prev.wait_send)

    @pl.when(has_next)
    def _():
        to_next.wait_send()
        ext_next.wait_send()

    pl.when(k < depths - 1)(z_back.wait_send)
    pl.when(k > 0)(z_front.wait_send)
    for d in range(1, depths):
        to = lax.rem(k + d, depths)
        when_reduces(to, seg_copy(seg1_out, seg1_in, s1_send, s1_recv, d).wait_send)
        when_reduces(to, seg_copy(seg2_out, seg2_in, s2_send, s2_recv, d).wait_send)

    def sent_back():
        for d in range(1, depths):
            qd_copy(qd1_out, qd1_in, q1_send, q1_recv, d).wait_send()
            qd_copy(qd2_out, qd2_in, q2_send, q2_recv, d).wait_send()

        @pl.when(has_next)
        def _():
            for d in range(depths):
                qd_copy_next(d).wait_send()

    when_reduces(k, sent_back)


def gradient_of_loss(grid, ray_offset, occupancy, target, tiles, depths):
    channels, rows, planes, width = grid.shape
    pieces = max(1, min(depths, width // 128))
    piece = width // pieces
    f32 = jnp.float32
    vmem, dma = pltpu.VMEM, pltpu.SemaphoreType.DMA
    scratch = [
        vmem(grid.shape, f32), vmem(ray_offset.shape, jnp.int32), vmem(occupancy.shape, jnp.int32),
        vmem(target.shape, f32),
        vmem((channels, 1, planes, width), f32), vmem((channels, 1, planes, width), f32),
        vmem((8, width), f32), vmem((8, width), f32),
        vmem((2, channels * rows, width), f32), vmem((2, channels * rows, width), f32),
        vmem((rows + 1, 3, planes, width), f32), vmem((rows + 1, planes, width), f32),
        vmem((rows + 1, planes, width), f32), vmem((rows + 1, planes, width), f32),
    ]
    for count in (rows - 1, 1):
        scratch += [vmem((pieces, 4, count, piece), f32), vmem((depths, 4, count, piece), f32)]
    for count in (rows - 1, 1):
        scratch += [vmem((depths, 4, count, piece), f32), vmem((pieces, 4, count, piece), f32)]
    scratch += [vmem((pieces, 4, 1, piece), f32)]
    scratch += [dma((4,)), dma((5,)), dma((5,))] + [dma((depths,))] * 10
    hbm = pl.BlockSpec(memory_space=pltpu.HBM)
    return pl.pallas_call(
        functools.partial(kernel, tiles, depths, pieces),
        out_shape=pltpu.VMEM(grid.shape, f32),
        in_specs=[hbm] * 4,
        out_specs=pl.BlockSpec(memory_space=pltpu.VMEM),
        scratch_shapes=scratch,
        compiler_params=pltpu.CompilerParams(
            collective_id=0, has_side_effects=True, vmem_limit_bytes=24 * 2**20
        ),
        cost_estimate=pl.CostEstimate(flops=10**7, bytes_accessed=2**20, transcendentals=10**6),
    )(*(pltpu.with_memory_space_constraint(x, pltpu.HBM) for x in (grid, ray_offset, occupancy, target)))


def solution(mesh):
    tiles, depths = mesh.shape["tile"], mesh.shape["depth"]
    voxels = P(None, "tile", "depth", None)
    in_specs = (voxels, voxels, voxels, P("tile", None), P("tile", "depth", None), P(None, "tile", None))

    def body(grid, first_moment, second_moment, ray_offset, occupancy, target):
        grad = gradient_of_loss(grid, ray_offset, occupancy, target, tiles, depths)
        new_first = beta_one * first_moment + (1.0 - beta_one) * grad
        new_second = beta_two * second_moment + (1.0 - beta_two) * grad * grad
        corr_one = 1.0 - beta_one**adam_step
        corr_two = 1.0 - beta_two**adam_step
        new_grid = grid - learn_rate * (new_first / corr_one) / (jnp.sqrt(new_second / corr_two) + epsilon)
        return (new_grid, new_first, new_second)

    return jax.shard_map(body, mesh=mesh, in_specs=in_specs, out_specs=(voxels,) * 3, check_vma=False)
```

```python
import functools

import jax
import jax.numpy as jnp
from jax import lax
from jax.experimental import pallas as pl
from jax.experimental.pallas import tpu as pltpu
from jax.sharding import PartitionSpec as P

MESH = pl.DeviceIdType.MESH
tv_weight = 0.01
beta_one = 0.9
beta_two = 0.95
learn_rate = 0.1
adam_step = 10
epsilon = 1e-08


def running_sum(x, iota, backward):
    count = x.shape[0]
    step = 1
    while step < count:
        if backward:
            x = x + jnp.where(iota < count - step, pltpu.roll(x, count - step, 0), 0.0)
        else:
            x = x + jnp.where(iota >= step, pltpu.roll(x, step, 0), 0.0)
        step *= 2
    return x


def one_minus_exp(s):
    series = 1.0 / 120 - s * (1.0 / 720)
    for term in (1.0 / 24, 1.0 / 6, 0.5, 1.0):
        series = term - s * series
    return jnp.where(s < 0.25, s * series, 1.0 - jnp.exp(-s))


def sigmoid(x):
    return 1.0 / (1.0 + jnp.exp(-x))


def kernel(
    tiles, depths, pieces,
    grid_h, ray_h, occ_h, tgt_h, grad_ref,
    g, ray, occ_i, tgt, nxt, prv, ext_out, ext_in, zout, zin,
    col, wgt, ntr, dfac,
    seg1_out, seg1_in, seg2_out, seg2_in,
    qd1_out, qd1_in, qd2_out, qd2_in, qdp_in,
    load_sem, halo_send, halo_recv,
    s1_send, s1_recv, s2_send, s2_recv,
    q1_send, q1_recv, q2_send, q2_recv, qp_send, qp_recv,
):
    t, k = lax.axis_index("tile"), lax.axis_index("depth")
    channels, rows, planes, width = g.shape
    last = rows - 1
    piece = width // pieces
    scale = 4.0 / (planes * depths)
    has_prev, has_next = t > 0, t < tiles - 1
    reduces = k < pieces

    loads = [
        pltpu.make_async_copy(src, dst, load_sem.at[i])
        for i, (src, dst) in enumerate(((grid_h, g), (ray_h, ray), (occ_h, occ_i), (tgt_h, tgt)))
    ]
    for load in loads:
        load.start()

    barrier = pltpu.get_barrier_semaphore()
    for d in range(1, depths):
        pl.semaphore_signal(barrier, inc=1, device_id={"depth": lax.rem(k + d, depths)}, device_id_type=MESH)

    @pl.when(has_prev)
    def _():
        for j in range(depths):
            pl.semaphore_signal(barrier, inc=1, device_id={"tile": t - 1, "depth": j}, device_id_type=MESH)

    @pl.when(has_next)
    def _():
        for j in range(depths):
            pl.semaphore_signal(barrier, inc=1, device_id={"tile": t + 1, "depth": j}, device_id_type=MESH)

    @pl.when(jnp.logical_not(has_prev))
    def _():
        prv[...] = jnp.zeros_like(prv)
        ext_in[...] = jnp.zeros_like(ext_in)
        qdp_in[...] = jnp.zeros_like(qdp_in)

    @pl.when(jnp.logical_not(has_next))
    def _():
        nxt[...] = jnp.zeros_like(nxt)

    @pl.when(k == 0)
    def _():
        zin[0] = jnp.zeros(zin.shape[1:], jnp.float32)

    @pl.when(k == depths - 1)
    def _():
        zin[1] = jnp.zeros(zin.shape[1:], jnp.float32)

    to_prev = pltpu.make_async_remote_copy(
        grid_h.at[:, 0:1], nxt, halo_send.at[0], halo_recv.at[0], device_id={"tile": t - 1}, device_id_type=MESH
    )
    to_next = pltpu.make_async_remote_copy(
        g.at[:, last:rows], prv, halo_send.at[1], halo_recv.at[1], device_id={"tile": t + 1}, device_id_type=MESH
    )
    ext_next = pltpu.make_async_remote_copy(
        ext_out, ext_in, halo_send.at[2], halo_recv.at[2], device_id={"tile": t + 1}, device_id_type=MESH
    )
    z_back = pltpu.make_async_remote_copy(
        zout.at[0], zin.at[0], halo_send.at[3], halo_recv.at[3], device_id={"depth": k + 1}, device_id_type=MESH
    )
    z_front = pltpu.make_async_remote_copy(
        zout.at[1], zin.at[1], halo_send.at[4], halo_recv.at[4], device_id={"depth": k - 1}, device_id_type=MESH
    )

    partners = depths - 1 + depths * (has_prev.astype(jnp.int32) + has_next.astype(jnp.int32))
    pl.semaphore_wait(barrier, partners)

    @pl.when(has_prev)
    def _():
        to_prev.start()

    for load in loads:
        load.wait()

    blocks = occ_i.shape[2]
    spread = lax.broadcasted_iota(jnp.int32, (blocks, width), 1) // (width // blocks)
    spread = (spread == lax.broadcasted_iota(jnp.int32, (blocks, width), 0)).astype(jnp.float32)
    occ_rows = jnp.broadcast_to(occ_i[0].astype(jnp.float32), (8, blocks))
    occ = jnp.dot(occ_rows, spread, preferred_element_type=jnp.float32)[0:1]
    ext_out[0:1, :] = ray[last : last + 1, :].astype(jnp.float32) * 0.5
    ext_out[1:2, :] = occ
    @pl.when(has_next)
    def _():
        to_next.start()
        ext_next.start()

    for c in range(channels):
        for r in range(rows):
            zout[0, c * rows + r : c * rows + r + 1, :] = g[c, r, planes - 1 : planes, :]
            zout[1, c * rows + r : c * rows + r + 1, :] = g[c, r, 0:1, :]

    @pl.when(k < depths - 1)
    def _():
        z_back.start()

    @pl.when(k > 0)
    def _():
        z_front.start()

    planes_at = lax.broadcasted_iota(jnp.int32, (planes, width), 0)

    def samples(slot, here, after, share, occ):
        density = here(0) + share * (after(0) - here(0))
        tail = jnp.exp(-jnp.abs(density))
        sigma = occ * (jnp.maximum(density, 0.0) + jnp.log1p(tail)) * scale
        dfac[slot] = occ * scale * jnp.where(density >= 0.0, 1.0, tail) / (1.0 + tail)
        upto = running_sum(sigma, planes_at, False)
        weight = jnp.exp(sigma - upto) * one_minus_exp(sigma)
        after_all = jnp.exp(-upto)
        wgt[slot] = weight
        ntr[slot] = after_all
        out = []
        for c in range(1, channels):
            colour = sigmoid(here(c) + share * (after(c) - here(c)))
            col[slot, c - 1] = colour
            out.append(jnp.sum(weight * colour, axis=0, keepdims=True))
        out.append(after_all[planes - 1 : planes])
        return out

    def share_of(r):
        return ray[r : r + 1, :].astype(jnp.float32) * 0.5

    def put(seg_out, r, values):
        for v in range(channels):
            for p in range(pieces):
                seg_out[p, v, r : r + 1, :] = values[v][:, p * piece : (p + 1) * piece]

    def when_reduces(who, work):
        if pieces < depths:
            pl.when(who < pieces)(work)
        else:
            work()

    def seg_copy(seg_out, seg_in, send, recv, d, source=None):
        to = lax.rem(k + d, depths)
        slot = k if source is None else source
        return pltpu.make_async_remote_copy(
            seg_out.at[to % pieces], seg_in.at[slot], send.at[d], recv.at[slot],
            device_id={"depth": to}, device_id_type=MESH,
        )

    def send_segments(seg_out, seg_in, send, recv):
        for d in range(1, depths):
            when_reduces(lax.rem(k + d, depths), seg_copy(seg_out, seg_in, send, recv, d).start)

        def own():
            seg_in[k] = seg_out[k % pieces]

        when_reduces(k, own)

    def reduce(seg_in, qd_out, send, recv, first, count):
        for d in range(1, depths):
            source = lax.rem(k + d, depths)
            seg_copy(seg_in, seg_in, send, recv, d, source).wait_recv()
        at = pl.ds(pl.multiple_of((k % pieces) * piece, piece), piece)
        fronts = [None]
        front = seg_in[0, 3]
        pixel = [seg_in[0, c] for c in range(3)]
        fronts.append(front)
        for j in range(1, depths):
            for c in range(3):
                pixel[c] = pixel[c] + front * seg_in[j, c]
            front = front * seg_in[j, 3]
            fronts.append(front)
        half = 0.5 * planes * depths
        pg = [half * (pixel[c] + front - tgt[c, first : first + count, at]) for c in range(3)]
        behind = pg[0] + pg[1] + pg[2]
        for j in range(depths - 1, -1, -1):
            for c in range(3):
                qd_out[j, c] = pg[c] if j == 0 else fronts[j] * pg[c]
            qd_out[j, 3] = fronts[j + 1] * behind
            if j:
                behind = pg[0] * seg_in[j, 0] + pg[1] * seg_in[j, 1] + pg[2] * seg_in[j, 2] + seg_in[j, 3] * behind

    def qd_copy(qd_out, qd_in, send, recv, d, source=None):
        to = lax.rem(k + d, depths)
        slot = k % pieces if source is None else source % pieces
        return pltpu.make_async_remote_copy(
            qd_out.at[to], qd_in.at[slot], send.at[d], recv.at[slot],
            device_id={"depth": to}, device_id_type=MESH,
        )

    def qd_copy_next(d, source=None):
        to = lax.rem(k + d, depths)
        slot = k % pieces if source is None else source % pieces
        return pltpu.make_async_remote_copy(
            qd2_out.at[to], qdp_in.at[slot], qp_send.at[d], qp_recv.at[slot],
            device_id={"tile": t + 1, "depth": to}, device_id_type=MESH,
        )

    def send_back(qd_out, qd_in, send, recv):
        for d in range(1, depths):
            qd_copy(qd_out, qd_in, send, recv, d).start()
        qd_in[k % pieces] = qd_out[k]

    def wait_back(qd_in, send, recv):
        for d in range(1, depths):
            source = lax.rem(k + d, depths)
            when_reduces(source, qd_copy(qd_in, qd_in, send, recv, d, source).wait_recv)

    for r in range(last):
        values = samples(r, lambda c: g[c, r], lambda c: g[c, r + 1], share_of(r), occ)
        put(seg1_out, r, values)
    send_segments(seg1_out, seg1_in, s1_send, s1_recv)

    pl.when(has_next)(to_prev.wait_recv)
    values = samples(last, lambda c: g[c, last], lambda c: nxt[c, 0], share_of(last), occ)
    put(seg2_out, 0, values)
    send_segments(seg2_out, seg2_in, s2_send, s2_recv)

    def first_rows():
        reduce(seg1_in, qd1_out, s1_send, s1_recv, 0, last)
        send_back(qd1_out, qd1_in, q1_send, q1_recv)

    when_reduces(k, first_rows)

    lanes = lax.broadcasted_iota(jnp.int32, (planes, width), 1)
    for c in range(channels):
        for r in range(rows):
            here = g[c, r]
            around = jnp.where(planes_at == 0, 0.0, pltpu.roll(here, 1, 0))
            around += jnp.where(planes_at == planes - 1, 0.0, pltpu.roll(here, planes - 1, 0))
            around += jnp.where(lanes == 0, 0.0, pltpu.roll(here, 1, 1))
            around += jnp.where(lanes == width - 1, 0.0, pltpu.roll(here, width - 1, 1))
            if r > 0:
                around += g[c, r - 1]
            if r < last:
                around += g[c, r + 1]
            grad_ref[c, r] = 2.0 * tv_weight * (6.0 * here - around)

    def last_row():
        reduce(seg2_in, qd2_out, s2_send, s2_recv, last, 1)
        send_back(qd2_out, qd2_in, q2_send, q2_recv)

        @pl.when(has_next)
        def _():
            for d in range(depths):
                qd_copy_next(d).start()

    when_reduces(k, last_row)

    @pl.when(has_prev)
    def _():
        to_next.wait_recv()
        ext_next.wait_recv()

    samples(rows, lambda c: prv[c, 0], lambda c: g[c, 0], ext_in[0:1, :], ext_in[1:2, :])

    pl.when(k > 0)(z_back.wait_recv)
    pl.when(k < depths - 1)(z_front.wait_recv)
    for c in range(channels):
        for r in range(rows):
            i = c * rows + r
            grad_ref[c, r, 0:1, :] -= 2.0 * tv_weight * zin[0, i : i + 1, :]
            grad_ref[c, r, planes - 1 : planes, :] -= 2.0 * tv_weight * zin[1, i : i + 1, :]
        grad_ref[c, 0] -= 2.0 * tv_weight * prv[c, 0]
        grad_ref[c, last] -= 2.0 * tv_weight * nxt[c, 0]

    def gradient(slot, qd_in, r):
        q = [jnp.concatenate([qd_in[p, v, r : r + 1, :] for p in range(pieces)], axis=1) for v in range(4)]
        u = q[0] * col[slot, 0] + q[1] * col[slot, 1] + q[2] * col[slot, 2]
        weight = wgt[slot]
        part = weight * u
        rest = running_sum(part, planes_at, True) - part
        out = [(ntr[slot] * u - rest - q[3]) * dfac[slot]]
        for c in range(3):
            colour = col[slot, c]
            out.append(q[c] * weight * (colour * (1.0 - colour)))
        return out

    def add(r, factor, values):
        for c in range(channels):
            grad_ref[c, r] += factor * values[c]

    wait_back(qd1_in, q1_send, q1_recv)
    for r in range(last):
        values = gradient(r, qd1_in, r)
        add(r, 1.0 - share_of(r), values)
        add(r + 1, share_of(r), values)
    wait_back(qd2_in, q2_send, q2_recv)
    add(last, 1.0 - share_of(last), gradient(last, qd2_in, 0))

    @pl.when(has_prev)
    def _():
        for d in range(depths):
            source = lax.rem(k + d, depths)
            when_reduces(source, qd_copy_next(d, source).wait_recv)

    add(0, ext_in[0:1, :], gradient(rows, qdp_in, 0))

    pl.when(has_prev)(to_prev.wait_send)

    @pl.when(has_next)
    def _():
        to_next.wait_send()
        ext_next.wait_send()

    pl.when(k < depths - 1)(z_back.wait_send)
    pl.when(k > 0)(z_front.wait_send)
    for d in range(1, depths):
        to = lax.rem(k + d, depths)
        when_reduces(to, seg_copy(seg1_out, seg1_in, s1_send, s1_recv, d).wait_send)
        when_reduces(to, seg_copy(seg2_out, seg2_in, s2_send, s2_recv, d).wait_send)

    def sent_back():
        for d in range(1, depths):
            qd_copy(qd1_out, qd1_in, q1_send, q1_recv, d).wait_send()
            qd_copy(qd2_out, qd2_in, q2_send, q2_recv, d).wait_send()

        @pl.when(has_next)
        def _():
            for d in range(depths):
                qd_copy_next(d).wait_send()

    when_reduces(k, sent_back)


def gradient_of_loss(grid, ray_offset, occupancy, target, tiles, depths):
    channels, rows, planes, width = grid.shape
    pieces = max(1, min(depths, width // 128))
    piece = width // pieces
    f32 = jnp.float32
    vmem, dma = pltpu.VMEM, pltpu.SemaphoreType.DMA
    scratch = [
        vmem(grid.shape, f32), vmem(ray_offset.shape, jnp.int32), vmem(occupancy.shape, jnp.int32),
        vmem(target.shape, f32),
        vmem((channels, 1, planes, width), f32), vmem((channels, 1, planes, width), f32),
        vmem((8, width), f32), vmem((8, width), f32),
        vmem((2, channels * rows, width), f32), vmem((2, channels * rows, width), f32),
        vmem((rows + 1, 3, planes, width), f32), vmem((rows + 1, planes, width), f32),
        vmem((rows + 1, planes, width), f32), vmem((rows + 1, planes, width), f32),
    ]
    for count in (rows - 1, 1):
        scratch += [vmem((pieces, 4, count, piece), f32), vmem((depths, 4, count, piece), f32)]
    for count in (rows - 1, 1):
        scratch += [vmem((depths, 4, count, piece), f32), vmem((pieces, 4, count, piece), f32)]
    scratch += [vmem((pieces, 4, 1, piece), f32)]
    scratch += [dma((4,)), dma((5,)), dma((5,))] + [dma((depths,))] * 10
    hbm = pl.BlockSpec(memory_space=pltpu.HBM)
    return pl.pallas_call(
        functools.partial(kernel, tiles, depths, pieces),
        out_shape=pltpu.VMEM(grid.shape, f32),
        in_specs=[hbm] * 4,
        out_specs=pl.BlockSpec(memory_space=pltpu.VMEM),
        scratch_shapes=scratch,
        compiler_params=pltpu.CompilerParams(
            collective_id=0, has_side_effects=True, vmem_limit_bytes=24 * 2**20
        ),
        cost_estimate=pl.CostEstimate(flops=10**7, bytes_accessed=2**20, transcendentals=10**6),
    )(*(pltpu.with_memory_space_constraint(x, pltpu.HBM) for x in (grid, ray_offset, occupancy, target)))


def solution(mesh):
    tiles, depths = mesh.shape["tile"], mesh.shape["depth"]
    voxels = P(None, "tile", "depth", None)
    in_specs = (voxels, voxels, voxels, P("tile", None), P("tile", "depth", None), P(None, "tile", None))

    def body(grid, first_moment, second_moment, ray_offset, occupancy, target):
        grad = gradient_of_loss(grid, ray_offset, occupancy, target, tiles, depths)
        new_first = beta_one * first_moment + (1.0 - beta_one) * grad
        new_second = beta_two * second_moment + (1.0 - beta_two) * grad * grad
        corr_one = 1.0 - beta_one**adam_step
        corr_two = 1.0 - beta_two**adam_step
        new_grid = grid - learn_rate * (new_first / corr_one) / (jnp.sqrt(new_second / corr_two) + epsilon)
        return (new_grid, new_first, new_second)

    return jax.shard_map(body, mesh=mesh, in_specs=in_specs, out_specs=(voxels,) * 3, check_vma=False)
```

```python
import functools

import jax
import jax.numpy as jnp
from jax import lax
from jax.experimental import pallas as pl
from jax.experimental.pallas import tpu as pltpu
from jax.sharding import PartitionSpec as P

MESH = pl.DeviceIdType.MESH
tv_weight = 0.01
beta_one = 0.9
beta_two = 0.95
learn_rate = 0.1
adam_step = 10
epsilon = 1e-08


def running_sum(x, iota, backward):
    count = x.shape[0]
    step = 1
    while step < count:
        if backward:
            x = x + jnp.where(iota < count - step, pltpu.roll(x, count - step, 0), 0.0)
        else:
            x = x + jnp.where(iota >= step, pltpu.roll(x, step, 0), 0.0)
        step *= 2
    return x


def one_minus_exp(s):
    series = 1.0 / 120 - s * (1.0 / 720)
    for term in (1.0 / 24, 1.0 / 6, 0.5, 1.0):
        series = term - s * series
    return jnp.where(s < 0.25, s * series, 1.0 - jnp.exp(-s))


def sigmoid(x):
    return 1.0 / (1.0 + jnp.exp(-x))


def kernel(
    tiles, depths, pieces,
    grid_h, ray_h, occ_h, tgt_h, grad_ref,
    g, ray, occ_i, tgt, nxt, prv, ext_out, ext_in, zout, zin,
    col, wgt, ntr, dfac,
    seg1_out, seg1_in, seg2_out, seg2_in,
    qd1_out, qd1_in, qd2_out, qd2_in,
    load_sem, halo_send, halo_recv,
    s1_send, s1_recv, s2_send, s2_recv,
    q1_send, q1_recv, q2_send, q2_recv,
):
    t, k = lax.axis_index("tile"), lax.axis_index("depth")
    channels, rows, planes, width = g.shape
    last = rows - 1
    piece = width // pieces
    scale = 4.0 / (planes * depths)
    has_prev, has_next = t > 0, t < tiles - 1
    reduces = k < pieces

    loads = [
        pltpu.make_async_copy(src, dst, load_sem.at[i])
        for i, (src, dst) in enumerate(((grid_h, g), (ray_h, ray), (occ_h, occ_i), (tgt_h, tgt)))
    ]
    for load in loads:
        load.start()

    barrier = pltpu.get_barrier_semaphore()
    for d in range(1, depths):
        pl.semaphore_signal(barrier, inc=1, device_id={"depth": lax.rem(k + d, depths)}, device_id_type=MESH)

    @pl.when(has_prev)
    def _():
        pl.semaphore_signal(barrier, inc=1, device_id={"tile": t - 1}, device_id_type=MESH)

    @pl.when(has_next)
    def _():
        pl.semaphore_signal(barrier, inc=1, device_id={"tile": t + 1}, device_id_type=MESH)

    @pl.when(jnp.logical_not(has_prev))
    def _():
        prv[...] = jnp.zeros_like(prv)
        ext_in[...] = jnp.zeros_like(ext_in)

    @pl.when(jnp.logical_not(has_next))
    def _():
        nxt[...] = jnp.zeros_like(nxt)

    @pl.when(k == 0)
    def _():
        zin[0] = jnp.zeros(zin.shape[1:], jnp.float32)

    @pl.when(k == depths - 1)
    def _():
        zin[1] = jnp.zeros(zin.shape[1:], jnp.float32)

    to_prev = pltpu.make_async_remote_copy(
        grid_h.at[:, 0:1], nxt, halo_send.at[0], halo_recv.at[0], device_id={"tile": t - 1}, device_id_type=MESH
    )
    to_next = pltpu.make_async_remote_copy(
        grid_h.at[:, last:rows], prv, halo_send.at[1], halo_recv.at[1], device_id={"tile": t + 1}, device_id_type=MESH
    )
    ext_next = pltpu.make_async_remote_copy(
        ext_out, ext_in, halo_send.at[2], halo_recv.at[2], device_id={"tile": t + 1}, device_id_type=MESH
    )
    z_back = pltpu.make_async_remote_copy(
        zout.at[0], zin.at[0], halo_send.at[3], halo_recv.at[3], device_id={"depth": k + 1}, device_id_type=MESH
    )
    z_front = pltpu.make_async_remote_copy(
        zout.at[1], zin.at[1], halo_send.at[4], halo_recv.at[4], device_id={"depth": k - 1}, device_id_type=MESH
    )

    partners = depths - 1 + has_prev.astype(jnp.int32) + has_next.astype(jnp.int32)
    pl.semaphore_wait(barrier, partners)

    @pl.when(has_prev)
    def _():
        to_prev.start()

    @pl.when(has_next)
    def _():
        to_next.start()

    for load in loads:
        load.wait()

    blocks = occ_i.shape[2]
    spread = lax.broadcasted_iota(jnp.int32, (blocks, width), 1) // (width // blocks)
    spread = (spread == lax.broadcasted_iota(jnp.int32, (blocks, width), 0)).astype(jnp.float32)
    occ_rows = jnp.broadcast_to(occ_i[0].astype(jnp.float32), (8, blocks))
    occ = jnp.dot(occ_rows, spread, preferred_element_type=jnp.float32)[0:1]
    ext_out[0:1, :] = ray[last : last + 1, :].astype(jnp.float32) * 0.5
    ext_out[1:2, :] = occ
    for c in range(3):
        ext_out[2 + c : 3 + c, :] = tgt[c, last : last + 1, :]
    @pl.when(has_next)
    def _():
        ext_next.start()

    for c in range(channels):
        for r in range(rows):
            zout[0, c * rows + r : c * rows + r + 1, :] = g[c, r, planes - 1 : planes, :]
            zout[1, c * rows + r : c * rows + r + 1, :] = g[c, r, 0:1, :]

    @pl.when(k < depths - 1)
    def _():
        z_back.start()

    @pl.when(k > 0)
    def _():
        z_front.start()

    planes_at = lax.broadcasted_iota(jnp.int32, (planes, width), 0)

    def samples(slot, here, after, share, occ):
        density = here(0) + share * (after(0) - here(0))
        tail = jnp.exp(-jnp.abs(density))
        sigma = occ * (jnp.maximum(density, 0.0) + jnp.log1p(tail)) * scale
        dfac[slot] = occ * scale * jnp.where(density >= 0.0, 1.0, tail) / (1.0 + tail)
        upto = running_sum(sigma, planes_at, False)
        weight = jnp.exp(sigma - upto) * one_minus_exp(sigma)
        after_all = jnp.exp(-upto)
        wgt[slot] = weight
        ntr[slot] = after_all
        out = []
        for c in range(1, channels):
            colour = sigmoid(here(c) + share * (after(c) - here(c)))
            col[slot, c - 1] = colour
            out.append(jnp.sum(weight * colour, axis=0, keepdims=True))
        out.append(after_all[planes - 1 : planes])
        return out

    def share_of(r):
        return ray[r : r + 1, :].astype(jnp.float32) * 0.5

    def put(seg_out, r, values):
        for v in range(channels):
            for p in range(pieces):
                seg_out[p, v, r : r + 1, :] = values[v][:, p * piece : (p + 1) * piece]

    def when_reduces(who, work):
        if pieces < depths:
            pl.when(who < pieces)(work)
        else:
            work()

    def seg_copy(seg_out, seg_in, send, recv, d, source=None):
        to = lax.rem(k + d, depths)
        slot = k if source is None else source
        return pltpu.make_async_remote_copy(
            seg_out.at[to % pieces], seg_in.at[slot], send.at[d], recv.at[slot],
            device_id={"depth": to}, device_id_type=MESH,
        )

    def send_segments(seg_out, seg_in, send, recv):
        for d in range(1, depths):
            when_reduces(lax.rem(k + d, depths), seg_copy(seg_out, seg_in, send, recv, d).start)

        def own():
            seg_in[k] = seg_out[k % pieces]

        when_reduces(k, own)

    def reduce(seg_in, qd_out, send, recv, wanted):
        for d in range(1, depths):
            source = lax.rem(k + d, depths)
            seg_copy(seg_in, seg_in, send, recv, d, source).wait_recv()
        at = pl.ds(pl.multiple_of((k % pieces) * piece, piece), piece)
        fronts = [None]
        front = seg_in[0, 3]
        pixel = [seg_in[0, c] for c in range(3)]
        fronts.append(front)
        for j in range(1, depths):
            for c in range(3):
                pixel[c] = pixel[c] + front * seg_in[j, c]
            front = front * seg_in[j, 3]
            fronts.append(front)
        half = 0.5 * planes * depths
        pg = [half * (pixel[c] + front - wanted(c, at)) for c in range(3)]
        behind = pg[0] + pg[1] + pg[2]
        for j in range(depths - 1, -1, -1):
            for c in range(3):
                qd_out[j, c] = pg[c] if j == 0 else fronts[j] * pg[c]
            qd_out[j, 3] = fronts[j + 1] * behind
            if j:
                behind = pg[0] * seg_in[j, 0] + pg[1] * seg_in[j, 1] + pg[2] * seg_in[j, 2] + seg_in[j, 3] * behind

    def qd_copy(qd_out, qd_in, send, recv, d, source=None):
        to = lax.rem(k + d, depths)
        slot = k % pieces if source is None else source % pieces
        return pltpu.make_async_remote_copy(
            qd_out.at[to], qd_in.at[slot], send.at[d], recv.at[slot],
            device_id={"depth": to}, device_id_type=MESH,
        )

    def send_back(qd_out, qd_in, send, recv):
        for d in range(1, depths):
            qd_copy(qd_out, qd_in, send, recv, d).start()
        qd_in[k % pieces] = qd_out[k]

    def wait_back(qd_in, send, recv):
        for d in range(1, depths):
            source = lax.rem(k + d, depths)
            when_reduces(source, qd_copy(qd_in, qd_in, send, recv, d, source).wait_recv)

    for r in range(last):
        values = samples(r, lambda c: g[c, r], lambda c: g[c, r + 1], share_of(r), occ)
        put(seg1_out, r, values)
    send_segments(seg1_out, seg1_in, s1_send, s1_recv)

    pl.when(has_next)(to_prev.wait_recv)
    values = samples(last, lambda c: g[c, last], lambda c: nxt[c, 0], share_of(last), occ)
    put(seg2_out, 0, values)

    @pl.when(has_prev)
    def _():
        to_next.wait_recv()
        ext_next.wait_recv()

    values = samples(rows, lambda c: prv[c, 0], lambda c: g[c, 0], ext_in[0:1, :], ext_in[1:2, :])
    put(seg2_out, 1, values)
    send_segments(seg2_out, seg2_in, s2_send, s2_recv)

    def first_rows():
        reduce(seg1_in, qd1_out, s1_send, s1_recv, lambda c, at: tgt[c, 0:last, at])
        send_back(qd1_out, qd1_in, q1_send, q1_recv)

    when_reduces(k, first_rows)

    lanes = lax.broadcasted_iota(jnp.int32, (planes, width), 1)
    for c in range(channels):
        for r in range(rows):
            here = g[c, r]
            around = jnp.where(planes_at == 0, 0.0, pltpu.roll(here, 1, 0))
            around += jnp.where(planes_at == planes - 1, 0.0, pltpu.roll(here, planes - 1, 0))
            around += jnp.where(lanes == 0, 0.0, pltpu.roll(here, 1, 1))
            around += jnp.where(lanes == width - 1, 0.0, pltpu.roll(here, width - 1, 1))
            if r > 0:
                around += g[c, r - 1]
            if r < last:
                around += g[c, r + 1]
            grad_ref[c, r] = 2.0 * tv_weight * (6.0 * here - around)

    def last_row():
        reduce(
            seg2_in, qd2_out, s2_send, s2_recv,
            lambda c, at: jnp.concatenate([tgt[c, last:rows, at], ext_in[2 + c : 3 + c, at]], axis=0),
        )
        send_back(qd2_out, qd2_in, q2_send, q2_recv)

    when_reduces(k, last_row)

    pl.when(k > 0)(z_back.wait_recv)
    pl.when(k < depths - 1)(z_front.wait_recv)
    for c in range(channels):
        for r in range(rows):
            i = c * rows + r
            grad_ref[c, r, 0:1, :] -= 2.0 * tv_weight * zin[0, i : i + 1, :]
            grad_ref[c, r, planes - 1 : planes, :] -= 2.0 * tv_weight * zin[1, i : i + 1, :]
        grad_ref[c, 0] -= 2.0 * tv_weight * prv[c, 0]
        grad_ref[c, last] -= 2.0 * tv_weight * nxt[c, 0]

    def gradient(slot, qd_in, r):
        q = [jnp.concatenate([qd_in[p, v, r : r + 1, :] for p in range(pieces)], axis=1) for v in range(4)]
        u = q[0] * col[slot, 0] + q[1] * col[slot, 1] + q[2] * col[slot, 2]
        weight = wgt[slot]
        part = weight * u
        rest = running_sum(part, planes_at, True) - part
        out = [(ntr[slot] * u - rest - q[3]) * dfac[slot]]
        for c in range(3):
            colour = col[slot, c]
            out.append(q[c] * weight * (colour * (1.0 - colour)))
        return out

    def add(r, factor, values):
        for c in range(channels):
            grad_ref[c, r] += factor * values[c]

    wait_back(qd1_in, q1_send, q1_recv)
    for r in range(last):
        values = gradient(r, qd1_in, r)
        add(r, 1.0 - share_of(r), values)
        add(r + 1, share_of(r), values)
    wait_back(qd2_in, q2_send, q2_recv)
    add(last, 1.0 - share_of(last), gradient(last, qd2_in, 0))

    add(0, ext_in[0:1, :], gradient(rows, qd2_in, 1))

    pl.when(has_prev)(to_prev.wait_send)

    @pl.when(has_next)
    def _():
        to_next.wait_send()
        ext_next.wait_send()

    pl.when(k < depths - 1)(z_back.wait_send)
    pl.when(k > 0)(z_front.wait_send)
    for d in range(1, depths):
        to = lax.rem(k + d, depths)
        when_reduces(to, seg_copy(seg1_out, seg1_in, s1_send, s1_recv, d).wait_send)
        when_reduces(to, seg_copy(seg2_out, seg2_in, s2_send, s2_recv, d).wait_send)

    def sent_back():
        for d in range(1, depths):
            qd_copy(qd1_out, qd1_in, q1_send, q1_recv, d).wait_send()
            qd_copy(qd2_out, qd2_in, q2_send, q2_recv, d).wait_send()

    when_reduces(k, sent_back)


def gradient_of_loss(grid, ray_offset, occupancy, target, tiles, depths):
    channels, rows, planes, width = grid.shape
    pieces = max(1, min(depths, width // 128))
    piece = width // pieces
    f32 = jnp.float32
    vmem, dma = pltpu.VMEM, pltpu.SemaphoreType.DMA
    scratch = [
        vmem(grid.shape, f32), vmem(ray_offset.shape, jnp.int32), vmem(occupancy.shape, jnp.int32),
        vmem(target.shape, f32),
        vmem((channels, 1, planes, width), f32), vmem((channels, 1, planes, width), f32),
        vmem((8, width), f32), vmem((8, width), f32),
        vmem((2, channels * rows, width), f32), vmem((2, channels * rows, width), f32),
        vmem((rows + 1, 3, planes, width), f32), vmem((rows + 1, planes, width), f32),
        vmem((rows + 1, planes, width), f32), vmem((rows + 1, planes, width), f32),
    ]
    for count in (rows - 1, 2):
        scratch += [vmem((pieces, 4, count, piece), f32), vmem((depths, 4, count, piece), f32)]
    for count in (rows - 1, 2):
        scratch += [vmem((depths, 4, count, piece), f32), vmem((pieces, 4, count, piece), f32)]
    scratch += [dma((4,)), dma((5,)), dma((5,))] + [dma((depths,))] * 8
    hbm = pl.BlockSpec(memory_space=pltpu.HBM)
    return pl.pallas_call(
        functools.partial(kernel, tiles, depths, pieces),
        out_shape=pltpu.VMEM(grid.shape, f32),
        in_specs=[hbm] * 4,
        out_specs=pl.BlockSpec(memory_space=pltpu.VMEM),
        scratch_shapes=scratch,
        compiler_params=pltpu.CompilerParams(
            collective_id=0, has_side_effects=True, vmem_limit_bytes=24 * 2**20
        ),
        cost_estimate=pl.CostEstimate(flops=10**7, bytes_accessed=2**20, transcendentals=10**6),
    )(*(pltpu.with_memory_space_constraint(x, pltpu.HBM) for x in (grid, ray_offset, occupancy, target)))


def solution(mesh):
    tiles, depths = mesh.shape["tile"], mesh.shape["depth"]
    voxels = P(None, "tile", "depth", None)
    in_specs = (voxels, voxels, voxels, P("tile", None), P("tile", "depth", None), P(None, "tile", None))

    def body(grid, first_moment, second_moment, ray_offset, occupancy, target):
        grad = gradient_of_loss(grid, ray_offset, occupancy, target, tiles, depths)
        new_first = beta_one * first_moment + (1.0 - beta_one) * grad
        new_second = beta_two * second_moment + (1.0 - beta_two) * grad * grad
        corr_one = 1.0 - beta_one**adam_step
        corr_two = 1.0 - beta_two**adam_step
        new_grid = grid - learn_rate * (new_first / corr_one) / (jnp.sqrt(new_second / corr_two) + epsilon)
        return (new_grid, new_first, new_second)

    return jax.shard_map(body, mesh=mesh, in_specs=in_specs, out_specs=(voxels,) * 3, check_vma=False)
```

```python
import functools

import jax
import jax.numpy as jnp
from jax import lax
from jax.experimental import pallas as pl
from jax.experimental.pallas import tpu as pltpu
from jax.sharding import PartitionSpec as P

MESH = pl.DeviceIdType.MESH
tv_weight = 0.01
beta_one = 0.9
beta_two = 0.95
learn_rate = 0.1
adam_step = 10
epsilon = 1e-08


def running_sum(x, iota, backward):
    count = x.shape[0]
    step = 1
    while step < count:
        if backward:
            x = x + jnp.where(iota < count - step, pltpu.roll(x, count - step, 0), 0.0)
        else:
            x = x + jnp.where(iota >= step, pltpu.roll(x, step, 0), 0.0)
        step *= 2
    return x


def one_minus_exp(s):
    series = 1.0 / 120 - s * (1.0 / 720)
    for term in (1.0 / 24, 1.0 / 6, 0.5, 1.0):
        series = term - s * series
    return jnp.where(s < 0.25, s * series, 1.0 - jnp.exp(-s))


def sigmoid(x):
    return 1.0 / (1.0 + jnp.exp(-x))


def kernel(
    tiles, depths, pieces,
    grid_h, ray_h, occ_h, tgt_h, grad_ref,
    g, ray, occ_i, tgt, nxt, prv, ext_out, ext_in, zout, zin,
    col, wgt, ntr, dfac,
    seg1_out, seg1_in, seg2_out, seg2_in,
    qd1_out, qd1_in, qd2_out, qd2_in, qdp_in,
    load_sem, halo_send, halo_recv,
    s1_send, s1_recv, s2_send, s2_recv,
    q1_send, q1_recv, q2_send, q2_recv, qp_send, qp_recv,
):
    t, k = lax.axis_index("tile"), lax.axis_index("depth")
    channels, rows, planes, width = g.shape
    last = rows - 1
    piece = width // pieces
    scale = 4.0 / (planes * depths)
    has_prev, has_next = t > 0, t < tiles - 1
    reduces = k < pieces

    loads = [
        pltpu.make_async_copy(src, dst, load_sem.at[i])
        for i, (src, dst) in enumerate(((grid_h, g), (ray_h, ray), (occ_h, occ_i), (tgt_h, tgt)))
    ]
    for load in loads:
        load.start()

    barrier = pltpu.get_barrier_semaphore()
    for d in range(1, depths):
        pl.semaphore_signal(barrier, inc=1, device_id={"depth": lax.rem(k + d, depths)}, device_id_type=MESH)

    @pl.when(has_prev)
    def _():
        for j in range(depths):
            pl.semaphore_signal(barrier, inc=1, device_id={"tile": t - 1, "depth": j}, device_id_type=MESH)

    @pl.when(has_next)
    def _():
        for j in range(depths):
            pl.semaphore_signal(barrier, inc=1, device_id={"tile": t + 1, "depth": j}, device_id_type=MESH)

    @pl.when(jnp.logical_not(has_prev))
    def _():
        prv[...] = jnp.zeros_like(prv)
        ext_in[...] = jnp.zeros_like(ext_in)
        qdp_in[...] = jnp.zeros_like(qdp_in)

    @pl.when(jnp.logical_not(has_next))
    def _():
        nxt[...] = jnp.zeros_like(nxt)

    @pl.when(k == 0)
    def _():
        zin[0] = jnp.zeros(zin.shape[1:], jnp.float32)

    @pl.when(k == depths - 1)
    def _():
        zin[1] = jnp.zeros(zin.shape[1:], jnp.float32)

    to_prev = pltpu.make_async_remote_copy(
        grid_h.at[:, 0:1], nxt, halo_send.at[0], halo_recv.at[0], device_id={"tile": t - 1}, device_id_type=MESH
    )
    to_next = pltpu.make_async_remote_copy(
        g.at[:, last:rows], prv, halo_send.at[1], halo_recv.at[1], device_id={"tile": t + 1}, device_id_type=MESH
    )
    ext_next = pltpu.make_async_remote_copy(
        ext_out, ext_in, halo_send.at[2], halo_recv.at[2], device_id={"tile": t + 1}, device_id_type=MESH
    )
    z_back = pltpu.make_async_remote_copy(
        zout.at[0], zin.at[0], halo_send.at[3], halo_recv.at[3], device_id={"depth": k + 1}, device_id_type=MESH
    )
    z_front = pltpu.make_async_remote_copy(
        zout.at[1], zin.at[1], halo_send.at[4], halo_recv.at[4], device_id={"depth": k - 1}, device_id_type=MESH
    )

    partners = depths - 1 + depths * (has_prev.astype(jnp.int32) + has_next.astype(jnp.int32))
    pl.semaphore_wait(barrier, partners)

    @pl.when(has_prev)
    def _():
        to_prev.start()

    for load in loads:
        load.wait()

    blocks = occ_i.shape[2]
    spread = lax.broadcasted_iota(jnp.int32, (blocks, width), 1) // (width // blocks)
    spread = (spread == lax.broadcasted_iota(jnp.int32, (blocks, width), 0)).astype(jnp.float32)
    occ_rows = jnp.broadcast_to(occ_i[0].astype(jnp.float32), (8, blocks))
    occ = jnp.dot(occ_rows, spread, preferred_element_type=jnp.float32)[0:1]
    ext_out[0:1, :] = ray[last : last + 1, :].astype(jnp.float32) * 0.5
    ext_out[1:2, :] = occ
    for c in range(channels):
        for r in range(rows):
            zout[0, c * rows + r : c * rows + r + 1, :] = g[c, r, planes - 1 : planes, :]
            zout[1, c * rows + r : c * rows + r + 1, :] = g[c, r, 0:1, :]

    @pl.when(k < depths - 1)
    def _():
        z_back.start()

    @pl.when(k > 0)
    def _():
        z_front.start()

    planes_at = lax.broadcasted_iota(jnp.int32, (planes, width), 0)

    def samples(slot, here, after, share, occ):
        density = here(0) + share * (after(0) - here(0))
        tail = jnp.exp(-jnp.abs(density))
        sigma = occ * (jnp.maximum(density, 0.0) + jnp.log1p(tail)) * scale
        dfac[slot] = occ * scale * jnp.where(density >= 0.0, 1.0, tail) / (1.0 + tail)
        upto = running_sum(sigma, planes_at, False)
        weight = jnp.exp(sigma - upto) * one_minus_exp(sigma)
        after_all = jnp.exp(-upto)
        wgt[slot] = weight
        ntr[slot] = after_all
        out = []
        for c in range(1, channels):
            colour = sigmoid(here(c) + share * (after(c) - here(c)))
            col[slot, c - 1] = colour
            out.append(jnp.sum(weight * colour, axis=0, keepdims=True))
        out.append(after_all[planes - 1 : planes])
        return out

    def share_of(r):
        return ray[r : r + 1, :].astype(jnp.float32) * 0.5

    def put(seg_out, r, values):
        for v in range(channels):
            for p in range(pieces):
                seg_out[p, v, r : r + 1, :] = values[v][:, p * piece : (p + 1) * piece]

    def when_reduces(who, work):
        if pieces < depths:
            pl.when(who < pieces)(work)
        else:
            work()

    def seg_copy(seg_out, seg_in, send, recv, d, source=None):
        to = lax.rem(k + d, depths)
        slot = k if source is None else source
        return pltpu.make_async_remote_copy(
            seg_out.at[to % pieces], seg_in.at[slot], send.at[d], recv.at[slot],
            device_id={"depth": to}, device_id_type=MESH,
        )

    def send_segments(seg_out, seg_in, send, recv):
        for d in range(1, depths):
            when_reduces(lax.rem(k + d, depths), seg_copy(seg_out, seg_in, send, recv, d).start)

        def own():
            seg_in[k] = seg_out[k % pieces]

        when_reduces(k, own)

    def reduce(seg_in, qd_out, send, recv, first, count):
        for d in range(1, depths):
            source = lax.rem(k + d, depths)
            seg_copy(seg_in, seg_in, send, recv, d, source).wait_recv()
        at = pl.ds(pl.multiple_of((k % pieces) * piece, piece), piece)
        fronts = [None]
        front = seg_in[0, 3]
        pixel = [seg_in[0, c] for c in range(3)]
        fronts.append(front)
        for j in range(1, depths):
            for c in range(3):
                pixel[c] = pixel[c] + front * seg_in[j, c]
            front = front * seg_in[j, 3]
            fronts.append(front)
        half = 0.5 * planes * depths
        pg = [half * (pixel[c] + front - tgt[c, first : first + count, at]) for c in range(3)]
        behind = pg[0] + pg[1] + pg[2]
        for j in range(depths - 1, -1, -1):
            for c in range(3):
                qd_out[j, c] = pg[c] if j == 0 else fronts[j] * pg[c]
            qd_out[j, 3] = fronts[j + 1] * behind
            if j:
                behind = pg[0] * seg_in[j, 0] + pg[1] * seg_in[j, 1] + pg[2] * seg_in[j, 2] + seg_in[j, 3] * behind

    def qd_copy(qd_out, qd_in, send, recv, d, source=None):
        to = lax.rem(k + d, depths)
        slot = k % pieces if source is None else source % pieces
        return pltpu.make_async_remote_copy(
            qd_out.at[to], qd_in.at[slot], send.at[d], recv.at[slot],
            device_id={"depth": to}, device_id_type=MESH,
        )

    def qd_copy_next(d, source=None):
        to = lax.rem(k + d, depths)
        slot = k % pieces if source is None else source % pieces
        return pltpu.make_async_remote_copy(
            qd2_out.at[to], qdp_in.at[slot], qp_send.at[d], qp_recv.at[slot],
            device_id={"tile": t + 1, "depth": to}, device_id_type=MESH,
        )

    def send_back(qd_out, qd_in, send, recv):
        for d in range(1, depths):
            qd_copy(qd_out, qd_in, send, recv, d).start()
        qd_in[k % pieces] = qd_out[k]

    def wait_back(qd_in, send, recv):
        for d in range(1, depths):
            source = lax.rem(k + d, depths)
            when_reduces(source, qd_copy(qd_in, qd_in, send, recv, d, source).wait_recv)

    for r in range(last):
        values = samples(r, lambda c: g[c, r], lambda c: g[c, r + 1], share_of(r), occ)
        put(seg1_out, r, values)
    send_segments(seg1_out, seg1_in, s1_send, s1_recv)

    @pl.when(has_next)
    def _():
        to_prev.wait_recv()
        to_next.start()
        ext_next.start()

    values = samples(last, lambda c: g[c, last], lambda c: nxt[c, 0], share_of(last), occ)
    put(seg2_out, 0, values)
    send_segments(seg2_out, seg2_in, s2_send, s2_recv)

    def first_rows():
        reduce(seg1_in, qd1_out, s1_send, s1_recv, 0, last)
        send_back(qd1_out, qd1_in, q1_send, q1_recv)

    when_reduces(k, first_rows)

    lanes = lax.broadcasted_iota(jnp.int32, (planes, width), 1)
    for c in range(channels):
        for r in range(rows):
            here = g[c, r]
            around = jnp.where(planes_at == 0, 0.0, pltpu.roll(here, 1, 0))
            around += jnp.where(planes_at == planes - 1, 0.0, pltpu.roll(here, planes - 1, 0))
            around += jnp.where(lanes == 0, 0.0, pltpu.roll(here, 1, 1))
            around += jnp.where(lanes == width - 1, 0.0, pltpu.roll(here, width - 1, 1))
            if r > 0:
                around += g[c, r - 1]
            if r < last:
                around += g[c, r + 1]
            grad_ref[c, r] = 2.0 * tv_weight * (6.0 * here - around)

    def last_row():
        reduce(seg2_in, qd2_out, s2_send, s2_recv, last, 1)

        @pl.when(has_next)
        def _():
            for d in range(depths):
                qd_copy_next(d).start()

        send_back(qd2_out, qd2_in, q2_send, q2_recv)

    when_reduces(k, last_row)

    @pl.when(has_prev)
    def _():
        to_next.wait_recv()
        ext_next.wait_recv()

    samples(rows, lambda c: prv[c, 0], lambda c: g[c, 0], ext_in[0:1, :], ext_in[1:2, :])

    pl.when(k > 0)(z_back.wait_recv)
    pl.when(k < depths - 1)(z_front.wait_recv)
    for c in range(channels):
        for r in range(rows):
            i = c * rows + r
            grad_ref[c, r, 0:1, :] -= 2.0 * tv_weight * zin[0, i : i + 1, :]
            grad_ref[c, r, planes - 1 : planes, :] -= 2.0 * tv_weight * zin[1, i : i + 1, :]
        grad_ref[c, 0] -= 2.0 * tv_weight * prv[c, 0]
        grad_ref[c, last] -= 2.0 * tv_weight * nxt[c, 0]

    def gradient(slot, qd_in, r):
        q = [jnp.concatenate([qd_in[p, v, r : r + 1, :] for p in range(pieces)], axis=1) for v in range(4)]
        u = q[0] * col[slot, 0] + q[1] * col[slot, 1] + q[2] * col[slot, 2]
        weight = wgt[slot]
        part = weight * u
        rest = running_sum(part, planes_at, True) - part
        out = [(ntr[slot] * u - rest - q[3]) * dfac[slot]]
        for c in range(3):
            colour = col[slot, c]
            out.append(q[c] * weight * (colour * (1.0 - colour)))
        return out

    def add(r, factor, values):
        for c in range(channels):
            grad_ref[c, r] += factor * values[c]

    wait_back(qd1_in, q1_send, q1_recv)
    for r in range(last):
        values = gradient(r, qd1_in, r)
        add(r, 1.0 - share_of(r), values)
        add(r + 1, share_of(r), values)
    wait_back(qd2_in, q2_send, q2_recv)
    add(last, 1.0 - share_of(last), gradient(last, qd2_in, 0))

    @pl.when(has_prev)
    def _():
        for d in range(depths):
            source = lax.rem(k + d, depths)
            when_reduces(source, qd_copy_next(d, source).wait_recv)

    add(0, ext_in[0:1, :], gradient(rows, qdp_in, 0))

    pl.when(has_prev)(to_prev.wait_send)

    @pl.when(has_next)
    def _():
        to_next.wait_send()
        ext_next.wait_send()

    pl.when(k < depths - 1)(z_back.wait_send)
    pl.when(k > 0)(z_front.wait_send)
    for d in range(1, depths):
        to = lax.rem(k + d, depths)
        when_reduces(to, seg_copy(seg1_out, seg1_in, s1_send, s1_recv, d).wait_send)
        when_reduces(to, seg_copy(seg2_out, seg2_in, s2_send, s2_recv, d).wait_send)

    def sent_back():
        for d in range(1, depths):
            qd_copy(qd1_out, qd1_in, q1_send, q1_recv, d).wait_send()
            qd_copy(qd2_out, qd2_in, q2_send, q2_recv, d).wait_send()

        @pl.when(has_next)
        def _():
            for d in range(depths):
                qd_copy_next(d).wait_send()

    when_reduces(k, sent_back)


def gradient_of_loss(grid, ray_offset, occupancy, target, tiles, depths):
    channels, rows, planes, width = grid.shape
    pieces = max(1, min(depths, width // 128))
    piece = width // pieces
    f32 = jnp.float32
    vmem, dma = pltpu.VMEM, pltpu.SemaphoreType.DMA
    scratch = [
        vmem(grid.shape, f32), vmem(ray_offset.shape, jnp.int32), vmem(occupancy.shape, jnp.int32),
        vmem(target.shape, f32),
        vmem((channels, 1, planes, width), f32), vmem((channels, 1, planes, width), f32),
        vmem((8, width), f32), vmem((8, width), f32),
        vmem((2, channels * rows, width), f32), vmem((2, channels * rows, width), f32),
        vmem((rows + 1, 3, planes, width), f32), vmem((rows + 1, planes, width), f32),
        vmem((rows + 1, planes, width), f32), vmem((rows + 1, planes, width), f32),
    ]
    for count in (rows - 1, 1):
        scratch += [vmem((pieces, 4, count, piece), f32), vmem((depths, 4, count, piece), f32)]
    for count in (rows - 1, 1):
        scratch += [vmem((depths, 4, count, piece), f32), vmem((pieces, 4, count, piece), f32)]
    scratch += [vmem((pieces, 4, 1, piece), f32)]
    scratch += [dma((4,)), dma((5,)), dma((5,))] + [dma((depths,))] * 10
    hbm = pl.BlockSpec(memory_space=pltpu.HBM)
    return pl.pallas_call(
        functools.partial(kernel, tiles, depths, pieces),
        out_shape=pltpu.VMEM(grid.shape, f32),
        in_specs=[hbm] * 4,
        out_specs=pl.BlockSpec(memory_space=pltpu.VMEM),
        scratch_shapes=scratch,
        compiler_params=pltpu.CompilerParams(
            collective_id=0, has_side_effects=True, vmem_limit_bytes=24 * 2**20
        ),
        cost_estimate=pl.CostEstimate(flops=10**7, bytes_accessed=2**20, transcendentals=10**6),
    )(*(pltpu.with_memory_space_constraint(x, pltpu.HBM) for x in (grid, ray_offset, occupancy, target)))


def solution(mesh):
    tiles, depths = mesh.shape["tile"], mesh.shape["depth"]
    voxels = P(None, "tile", "depth", None)
    in_specs = (voxels, voxels, voxels, P("tile", None), P("tile", "depth", None), P(None, "tile", None))

    def body(grid, first_moment, second_moment, ray_offset, occupancy, target):
        grad = gradient_of_loss(grid, ray_offset, occupancy, target, tiles, depths)
        new_first = beta_one * first_moment + (1.0 - beta_one) * grad
        new_second = beta_two * second_moment + (1.0 - beta_two) * grad * grad
        corr_one = 1.0 - beta_one**adam_step
        corr_two = 1.0 - beta_two**adam_step
        new_grid = grid - learn_rate * (new_first / corr_one) / (jnp.sqrt(new_second / corr_two) + epsilon)
        return (new_grid, new_first, new_second)

    return jax.shard_map(body, mesh=mesh, in_specs=in_specs, out_specs=(voxels,) * 3, check_vma=False)
```

```python
import functools

import jax
import jax.numpy as jnp
from jax import lax
from jax.experimental import pallas as pl
from jax.experimental.pallas import tpu as pltpu
from jax.sharding import PartitionSpec as P

MESH = pl.DeviceIdType.MESH
tv_weight = 0.01
beta_one = 0.9
beta_two = 0.95
learn_rate = 0.1
adam_step = 10
epsilon = 1e-08


def running_sum(x, iota, backward):
    count = x.shape[0]
    step = 1
    while step < count:
        if backward:
            x = x + jnp.where(iota < count - step, pltpu.roll(x, count - step, 0), 0.0)
        else:
            x = x + jnp.where(iota >= step, pltpu.roll(x, step, 0), 0.0)
        step *= 2
    return x


def one_minus_exp(s):
    series = 1.0 / 120 - s * (1.0 / 720)
    for term in (1.0 / 24, 1.0 / 6, 0.5, 1.0):
        series = term - s * series
    return jnp.where(s < 0.25, s * series, 1.0 - jnp.exp(-s))


def sigmoid(x):
    return 1.0 / (1.0 + jnp.exp(-x))


def kernel(
    tiles, depths, pieces,
    grid_h, ray_h, occ_h, tgt_h, grad_ref,
    g, ray, occ_i, tgt, nxt, prv, ext_out, ext_in, zout, zin,
    col, wgt, ntr, dfac,
    seg1_out, seg1_in, seg2_out, seg2_in,
    qd1_out, qd1_in, qd2_out, qd2_in, qdp_in,
    load_sem, halo_send, halo_recv,
    s1_send, s1_recv, s2_send, s2_recv,
    q1_send, q1_recv, q2_send, q2_recv, qp_send, qp_recv,
):
    t, k = lax.axis_index("tile"), lax.axis_index("depth")
    channels, rows, planes, width = g.shape
    last = rows - 1
    piece = width // pieces
    scale = 4.0 / (planes * depths)
    has_prev, has_next = t > 0, t < tiles - 1
    reduces = k < pieces

    loads = [
        pltpu.make_async_copy(src, dst, load_sem.at[i])
        for i, (src, dst) in enumerate(((grid_h, g), (ray_h, ray), (occ_h, occ_i), (tgt_h, tgt)))
    ]
    for load in loads:
        load.start()

    barrier = pltpu.get_barrier_semaphore()
    for d in range(1, depths):
        pl.semaphore_signal(barrier, inc=1, device_id={"depth": lax.rem(k + d, depths)}, device_id_type=MESH)

    @pl.when(has_prev)
    def _():
        for j in range(depths):
            pl.semaphore_signal(barrier, inc=1, device_id={"tile": t - 1, "depth": j}, device_id_type=MESH)

    @pl.when(has_next)
    def _():
        for j in range(depths):
            pl.semaphore_signal(barrier, inc=1, device_id={"tile": t + 1, "depth": j}, device_id_type=MESH)

    @pl.when(jnp.logical_not(has_prev))
    def _():
        prv[...] = jnp.zeros_like(prv)
        ext_in[...] = jnp.zeros_like(ext_in)
        qdp_in[...] = jnp.zeros_like(qdp_in)

    @pl.when(jnp.logical_not(has_next))
    def _():
        nxt[...] = jnp.zeros_like(nxt)

    @pl.when(k == 0)
    def _():
        zin[0] = jnp.zeros(zin.shape[1:], jnp.float32)

    @pl.when(k == depths - 1)
    def _():
        zin[1] = jnp.zeros(zin.shape[1:], jnp.float32)

    to_prev = pltpu.make_async_remote_copy(
        grid_h.at[:, 0:1], nxt, halo_send.at[0], halo_recv.at[0], device_id={"tile": t - 1}, device_id_type=MESH
    )
    to_next = pltpu.make_async_remote_copy(
        g.at[:, last:rows], prv, halo_send.at[1], halo_recv.at[1], device_id={"tile": t + 1}, device_id_type=MESH
    )
    ext_next = pltpu.make_async_remote_copy(
        ext_out, ext_in, halo_send.at[2], halo_recv.at[2], device_id={"tile": t + 1}, device_id_type=MESH
    )
    z_back = pltpu.make_async_remote_copy(
        zout.at[0], zin.at[0], halo_send.at[3], halo_recv.at[3], device_id={"depth": k + 1}, device_id_type=MESH
    )
    z_front = pltpu.make_async_remote_copy(
        zout.at[1], zin.at[1], halo_send.at[4], halo_recv.at[4], device_id={"depth": k - 1}, device_id_type=MESH
    )

    partners = depths - 1 + depths * (has_prev.astype(jnp.int32) + has_next.astype(jnp.int32))
    pl.semaphore_wait(barrier, partners)

    @pl.when(has_prev)
    def _():
        to_prev.start()

    for load in loads:
        load.wait()

    blocks = occ_i.shape[2]
    spread = lax.broadcasted_iota(jnp.int32, (blocks, width), 1) // (width // blocks)
    spread = (spread == lax.broadcasted_iota(jnp.int32, (blocks, width), 0)).astype(jnp.float32)
    occ_rows = jnp.broadcast_to(occ_i[0].astype(jnp.float32), (8, blocks))
    occ = jnp.dot(occ_rows, spread, preferred_element_type=jnp.float32)[0:1]
    ext_out[0:1, :] = ray[last : last + 1, :].astype(jnp.float32) * 0.5
    ext_out[1:2, :] = occ
    for c in range(channels):
        for r in range(rows):
            zout[0, c * rows + r : c * rows + r + 1, :] = g[c, r, planes - 1 : planes, :]
            zout[1, c * rows + r : c * rows + r + 1, :] = g[c, r, 0:1, :]

    @pl.when(k < depths - 1)
    def _():
        z_back.start()

    @pl.when(k > 0)
    def _():
        z_front.start()

    planes_at = lax.broadcasted_iota(jnp.int32, (planes, width), 0)

    def samples(slot, here, after, share, occ):
        density = here(0) + share * (after(0) - here(0))
        tail = jnp.exp(-jnp.abs(density))
        sigma = occ * (jnp.maximum(density, 0.0) + jnp.log1p(tail)) * scale
        dfac[slot] = occ * scale * jnp.where(density >= 0.0, 1.0, tail) / (1.0 + tail)
        upto = running_sum(sigma, planes_at, False)
        weight = jnp.exp(sigma - upto) * one_minus_exp(sigma)
        after_all = jnp.exp(-upto)
        wgt[slot] = weight
        ntr[slot] = after_all
        out = []
        for c in range(1, channels):
            colour = sigmoid(here(c) + share * (after(c) - here(c)))
            col[slot, c - 1] = colour
            out.append(jnp.sum(weight * colour, axis=0, keepdims=True))
        out.append(after_all[planes - 1 : planes])
        return out

    def share_of(r):
        return ray[r : r + 1, :].astype(jnp.float32) * 0.5

    def put(seg_out, r, values):
        for v in range(channels):
            for p in range(pieces):
                seg_out[p, v, r : r + 1, :] = values[v][:, p * piece : (p + 1) * piece]

    def when_reduces(who, work):
        if pieces < depths:
            pl.when(who < pieces)(work)
        else:
            work()

    def seg_copy(seg_out, seg_in, send, recv, d, source=None):
        to = lax.rem(k + d, depths)
        slot = k if source is None else source
        return pltpu.make_async_remote_copy(
            seg_out.at[to % pieces], seg_in.at[slot], send.at[d], recv.at[slot],
            device_id={"depth": to}, device_id_type=MESH,
        )

    def send_segments(seg_out, seg_in, send, recv):
        for d in range(1, depths):
            when_reduces(lax.rem(k + d, depths), seg_copy(seg_out, seg_in, send, recv, d).start)

        def own():
            seg_in[k] = seg_out[k % pieces]

        when_reduces(k, own)

    def reduce(seg_in, qd_out, send, recv, first, count):
        for d in range(1, depths):
            source = lax.rem(k + d, depths)
            seg_copy(seg_in, seg_in, send, recv, d, source).wait_recv()
        at = pl.ds(pl.multiple_of((k % pieces) * piece, piece), piece)
        fronts = [None]
        front = seg_in[0, 3]
        pixel = [seg_in[0, c] for c in range(3)]
        fronts.append(front)
        for j in range(1, depths):
            for c in range(3):
                pixel[c] = pixel[c] + front * seg_in[j, c]
            front = front * seg_in[j, 3]
            fronts.append(front)
        half = 0.5 * planes * depths
        pg = [half * (pixel[c] + front - tgt[c, first : first + count, at]) for c in range(3)]
        behind = pg[0] + pg[1] + pg[2]
        for j in range(depths - 1, -1, -1):
            for c in range(3):
                qd_out[j, c] = pg[c] if j == 0 else fronts[j] * pg[c]
            qd_out[j, 3] = fronts[j + 1] * behind
            if j:
                behind = pg[0] * seg_in[j, 0] + pg[1] * seg_in[j, 1] + pg[2] * seg_in[j, 2] + seg_in[j, 3] * behind

    def qd_copy(qd_out, qd_in, send, recv, d, source=None):
        to = lax.rem(k + d, depths)
        slot = k % pieces if source is None else source % pieces
        return pltpu.make_async_remote_copy(
            qd_out.at[to], qd_in.at[slot], send.at[d], recv.at[slot],
            device_id={"depth": to}, device_id_type=MESH,
        )

    def qd_copy_next(d, source=None):
        to = lax.rem(k + d, depths)
        slot = k % pieces if source is None else source % pieces
        return pltpu.make_async_remote_copy(
            qd2_out.at[to], qdp_in.at[slot], qp_send.at[d], qp_recv.at[slot],
            device_id={"tile": t + 1, "depth": to}, device_id_type=MESH,
        )

    def send_back(qd_out, qd_in, send, recv):
        for d in range(1, depths):
            qd_copy(qd_out, qd_in, send, recv, d).start()
        qd_in[k % pieces] = qd_out[k]

    def wait_back(qd_in, send, recv):
        for d in range(1, depths):
            source = lax.rem(k + d, depths)
            when_reduces(source, qd_copy(qd_in, qd_in, send, recv, d, source).wait_recv)

    lanes = lax.broadcasted_iota(jnp.int32, (planes, width), 1)

    def smooth_within(c):
        for r in range(rows):
            here = g[c, r]
            around = jnp.where(planes_at == 0, 0.0, pltpu.roll(here, 1, 0))
            around += jnp.where(planes_at == planes - 1, 0.0, pltpu.roll(here, planes - 1, 0))
            around += jnp.where(lanes == 0, 0.0, pltpu.roll(here, 1, 1))
            around += jnp.where(lanes == width - 1, 0.0, pltpu.roll(here, width - 1, 1))
            if r > 0:
                around += g[c, r - 1]
            if r < last:
                around += g[c, r + 1]
            grad_ref[c, r] = 2.0 * tv_weight * (6.0 * here - around)

    for r in range(last):
        values = samples(r, lambda c: g[c, r], lambda c: g[c, r + 1], share_of(r), occ)
        put(seg1_out, r, values)
    send_segments(seg1_out, seg1_in, s1_send, s1_recv)

    for c in range(channels // 2):
        smooth_within(c)

    @pl.when(has_next)
    def _():
        to_prev.wait_recv()
        to_next.start()
        ext_next.start()

    values = samples(last, lambda c: g[c, last], lambda c: nxt[c, 0], share_of(last), occ)
    put(seg2_out, 0, values)
    send_segments(seg2_out, seg2_in, s2_send, s2_recv)

    def first_rows():
        reduce(seg1_in, qd1_out, s1_send, s1_recv, 0, last)
        send_back(qd1_out, qd1_in, q1_send, q1_recv)

    when_reduces(k, first_rows)

    for c in range(channels // 2, channels):
        smooth_within(c)

    def last_row():
        reduce(seg2_in, qd2_out, s2_send, s2_recv, last, 1)

        @pl.when(has_next)
        def _():
            for d in range(depths):
                qd_copy_next(d).start()

        send_back(qd2_out, qd2_in, q2_send, q2_recv)

    when_reduces(k, last_row)

    pl.when(k > 0)(z_back.wait_recv)
    pl.when(k < depths - 1)(z_front.wait_recv)
    for c in range(channels):
        for r in range(rows):
            i = c * rows + r
            grad_ref[c, r, 0:1, :] -= 2.0 * tv_weight * zin[0, i : i + 1, :]
            grad_ref[c, r, planes - 1 : planes, :] -= 2.0 * tv_weight * zin[1, i : i + 1, :]
        grad_ref[c, last] -= 2.0 * tv_weight * nxt[c, 0]

    def gradient(slot, qd_in, r):
        q = [jnp.concatenate([qd_in[p, v, r : r + 1, :] for p in range(pieces)], axis=1) for v in range(4)]
        u = q[0] * col[slot, 0] + q[1] * col[slot, 1] + q[2] * col[slot, 2]
        weight = wgt[slot]
        part = weight * u
        rest = running_sum(part, planes_at, True) - part
        out = [(ntr[slot] * u - rest - q[3]) * dfac[slot]]
        for c in range(3):
            colour = col[slot, c]
            out.append(q[c] * weight * (colour * (1.0 - colour)))
        return out

    def add(r, factor, values):
        for c in range(channels):
            grad_ref[c, r] += factor * values[c]

    wait_back(qd1_in, q1_send, q1_recv)
    for r in range(last):
        values = gradient(r, qd1_in, r)
        add(r, 1.0 - share_of(r), values)
        add(r + 1, share_of(r), values)
    @pl.when(has_prev)
    def _():
        to_next.wait_recv()
        ext_next.wait_recv()

    samples(rows, lambda c: prv[c, 0], lambda c: g[c, 0], ext_in[0:1, :], ext_in[1:2, :])
    for c in range(channels):
        grad_ref[c, 0] -= 2.0 * tv_weight * prv[c, 0]

    wait_back(qd2_in, q2_send, q2_recv)
    add(last, 1.0 - share_of(last), gradient(last, qd2_in, 0))

    @pl.when(has_prev)
    def _():
        for d in range(depths):
            source = lax.rem(k + d, depths)
            when_reduces(source, qd_copy_next(d, source).wait_recv)

    add(0, ext_in[0:1, :], gradient(rows, qdp_in, 0))

    pl.when(has_prev)(to_prev.wait_send)

    @pl.when(has_next)
    def _():
        to_next.wait_send()
        ext_next.wait_send()

    pl.when(k < depths - 1)(z_back.wait_send)
    pl.when(k > 0)(z_front.wait_send)
    for d in range(1, depths):
        to = lax.rem(k + d, depths)
        when_reduces(to, seg_copy(seg1_out, seg1_in, s1_send, s1_recv, d).wait_send)
        when_reduces(to, seg_copy(seg2_out, seg2_in, s2_send, s2_recv, d).wait_send)

    def sent_back():
        for d in range(1, depths):
            qd_copy(qd1_out, qd1_in, q1_send, q1_recv, d).wait_send()
            qd_copy(qd2_out, qd2_in, q2_send, q2_recv, d).wait_send()

        @pl.when(has_next)
        def _():
            for d in range(depths):
                qd_copy_next(d).wait_send()

    when_reduces(k, sent_back)


def gradient_of_loss(grid, ray_offset, occupancy, target, tiles, depths):
    channels, rows, planes, width = grid.shape
    pieces = max(1, min(depths, width // 128))
    piece = width // pieces
    f32 = jnp.float32
    vmem, dma = pltpu.VMEM, pltpu.SemaphoreType.DMA
    scratch = [
        vmem(grid.shape, f32), vmem(ray_offset.shape, jnp.int32), vmem(occupancy.shape, jnp.int32),
        vmem(target.shape, f32),
        vmem((channels, 1, planes, width), f32), vmem((channels, 1, planes, width), f32),
        vmem((8, width), f32), vmem((8, width), f32),
        vmem((2, channels * rows, width), f32), vmem((2, channels * rows, width), f32),
        vmem((rows + 1, 3, planes, width), f32), vmem((rows + 1, planes, width), f32),
        vmem((rows + 1, planes, width), f32), vmem((rows + 1, planes, width), f32),
    ]
    for count in (rows - 1, 1):
        scratch += [vmem((pieces, 4, count, piece), f32), vmem((depths, 4, count, piece), f32)]
    for count in (rows - 1, 1):
        scratch += [vmem((depths, 4, count, piece), f32), vmem((pieces, 4, count, piece), f32)]
    scratch += [vmem((pieces, 4, 1, piece), f32)]
    scratch += [dma((4,)), dma((5,)), dma((5,))] + [dma((depths,))] * 10
    hbm = pl.BlockSpec(memory_space=pltpu.HBM)
    return pl.pallas_call(
        functools.partial(kernel, tiles, depths, pieces),
        out_shape=pltpu.VMEM(grid.shape, f32),
        in_specs=[hbm] * 4,
        out_specs=pl.BlockSpec(memory_space=pltpu.VMEM),
        scratch_shapes=scratch,
        compiler_params=pltpu.CompilerParams(
            collective_id=0, has_side_effects=True, vmem_limit_bytes=24 * 2**20
        ),
        cost_estimate=pl.CostEstimate(flops=10**7, bytes_accessed=2**20, transcendentals=10**6),
    )(*(pltpu.with_memory_space_constraint(x, pltpu.HBM) for x in (grid, ray_offset, occupancy, target)))


def solution(mesh):
    tiles, depths = mesh.shape["tile"], mesh.shape["depth"]
    voxels = P(None, "tile", "depth", None)
    in_specs = (voxels, voxels, voxels, P("tile", None), P("tile", "depth", None), P(None, "tile", None))

    def body(grid, first_moment, second_moment, ray_offset, occupancy, target):
        grad = gradient_of_loss(grid, ray_offset, occupancy, target, tiles, depths)
        new_first = beta_one * first_moment + (1.0 - beta_one) * grad
        new_second = beta_two * second_moment + (1.0 - beta_two) * grad * grad
        corr_one = 1.0 - beta_one**adam_step
        corr_two = 1.0 - beta_two**adam_step
        new_grid = grid - learn_rate * (new_first / corr_one) / (jnp.sqrt(new_second / corr_two) + epsilon)
        return (new_grid, new_first, new_second)

    return jax.shard_map(body, mesh=mesh, in_specs=in_specs, out_specs=(voxels,) * 3, check_vma=False)
```

```python
import functools

import jax
import jax.numpy as jnp
from jax import lax
from jax.experimental import pallas as pl
from jax.experimental.pallas import tpu as pltpu
from jax.sharding import PartitionSpec as P

MESH = pl.DeviceIdType.MESH
tv_weight = 0.01
beta_one = 0.9
beta_two = 0.95
learn_rate = 0.1
adam_step = 10
epsilon = 1e-08


def running_sum(x, iota, backward):
    count = x.shape[0]
    step = 1
    while step < count:
        if backward:
            x = x + jnp.where(iota < count - step, pltpu.roll(x, count - step, 0), 0.0)
        else:
            x = x + jnp.where(iota >= step, pltpu.roll(x, step, 0), 0.0)
        step *= 2
    return x


def one_minus_exp(s):
    series = 1.0 / 120 - s * (1.0 / 720)
    for term in (1.0 / 24, 1.0 / 6, 0.5, 1.0):
        series = term - s * series
    return jnp.where(s < 0.25, s * series, 1.0 - jnp.exp(-s))


def sigmoid(x):
    return 1.0 / (1.0 + jnp.exp(-x))


def kernel(
    tiles, depths, pieces,
    grid_h, ray_h, occ_h, tgt_h, grad_ref,
    g, ray, occ_i, tgt, nxt, prv, ext_out, ext_in, zout, zin,
    col, wgt, ntr, dfac,
    seg1_out, seg1_in, seg2_out, seg2_in,
    qd1_out, qd1_in, qd2_out, qd2_in, qdp_in,
    load_sem, halo_send, halo_recv,
    s1_send, s1_recv, s2_send, s2_recv,
    q1_send, q1_recv, q2_send, q2_recv, qp_send, qp_recv,
):
    t, k = lax.axis_index("tile"), lax.axis_index("depth")
    channels, rows, planes, width = g.shape
    last = rows - 1
    piece = width // pieces
    scale = 4.0 / (planes * depths)
    has_prev, has_next = t > 0, t < tiles - 1
    reduces = k < pieces

    loads = [
        pltpu.make_async_copy(src, dst, load_sem.at[i])
        for i, (src, dst) in enumerate(((grid_h, g), (ray_h, ray), (occ_h, occ_i), (tgt_h, tgt)))
    ]
    for load in loads:
        load.start()

    barrier = pltpu.get_barrier_semaphore()
    for d in range(1, depths):
        pl.semaphore_signal(barrier, inc=1, device_id={"depth": lax.rem(k + d, depths)}, device_id_type=MESH)

    @pl.when(has_prev)
    def _():
        for j in range(depths):
            pl.semaphore_signal(barrier, inc=1, device_id={"tile": t - 1, "depth": j}, device_id_type=MESH)

    @pl.when(has_next)
    def _():
        for j in range(depths):
            pl.semaphore_signal(barrier, inc=1, device_id={"tile": t + 1, "depth": j}, device_id_type=MESH)

    @pl.when(jnp.logical_not(has_prev))
    def _():
        prv[...] = jnp.zeros_like(prv)
        ext_in[...] = jnp.zeros_like(ext_in)
        qdp_in[...] = jnp.zeros_like(qdp_in)

    @pl.when(jnp.logical_not(has_next))
    def _():
        nxt[...] = jnp.zeros_like(nxt)

    @pl.when(k == 0)
    def _():
        zin[0] = jnp.zeros(zin.shape[1:], jnp.float32)

    @pl.when(k == depths - 1)
    def _():
        zin[1] = jnp.zeros(zin.shape[1:], jnp.float32)

    to_prev = pltpu.make_async_remote_copy(
        grid_h.at[:, 0:1], nxt, halo_send.at[0], halo_recv.at[0], device_id={"tile": t - 1}, device_id_type=MESH
    )
    to_next = pltpu.make_async_remote_copy(
        g.at[:, last:rows], prv, halo_send.at[1], halo_recv.at[1], device_id={"tile": t + 1}, device_id_type=MESH
    )
    ext_next = pltpu.make_async_remote_copy(
        ext_out, ext_in, halo_send.at[2], halo_recv.at[2], device_id={"tile": t + 1}, device_id_type=MESH
    )
    z_back = pltpu.make_async_remote_copy(
        zout.at[0], zin.at[0], halo_send.at[3], halo_recv.at[3], device_id={"depth": k + 1}, device_id_type=MESH
    )
    z_front = pltpu.make_async_remote_copy(
        zout.at[1], zin.at[1], halo_send.at[4], halo_recv.at[4], device_id={"depth": k - 1}, device_id_type=MESH
    )

    partners = depths - 1 + depths * (has_prev.astype(jnp.int32) + has_next.astype(jnp.int32))
    pl.semaphore_wait(barrier, partners)

    @pl.when(has_prev)
    def _():
        to_prev.start()

    for load in loads:
        load.wait()

    blocks = occ_i.shape[2]
    spread = lax.broadcasted_iota(jnp.int32, (blocks, width), 1) // (width // blocks)
    spread = (spread == lax.broadcasted_iota(jnp.int32, (blocks, width), 0)).astype(jnp.float32)
    occ_rows = jnp.broadcast_to(occ_i[0].astype(jnp.float32), (8, blocks))
    occ = jnp.dot(occ_rows, spread, preferred_element_type=jnp.float32)[0:1]
    ext_out[0:1, :] = ray[last : last + 1, :].astype(jnp.float32) * 0.5
    ext_out[1:2, :] = occ
    for c in range(channels):
        for r in range(rows):
            zout[0, c * rows + r : c * rows + r + 1, :] = g[c, r, planes - 1 : planes, :]
            zout[1, c * rows + r : c * rows + r + 1, :] = g[c, r, 0:1, :]

    @pl.when(k < depths - 1)
    def _():
        z_back.start()

    @pl.when(k > 0)
    def _():
        z_front.start()

    planes_at = lax.broadcasted_iota(jnp.int32, (planes, width), 0)

    def samples(slot, here, after, share, occ):
        density = here(0) + share * (after(0) - here(0))
        tail = jnp.exp(-jnp.abs(density))
        sigma = occ * (jnp.maximum(density, 0.0) + jnp.log1p(tail)) * scale
        dfac[slot] = occ * scale * jnp.where(density >= 0.0, 1.0, tail) / (1.0 + tail)
        upto = running_sum(sigma, planes_at, False)
        weight = jnp.exp(sigma - upto) * one_minus_exp(sigma)
        after_all = jnp.exp(-upto)
        wgt[slot] = weight
        ntr[slot] = after_all
        out = []
        for c in range(1, channels):
            colour = sigmoid(here(c) + share * (after(c) - here(c)))
            col[slot, c - 1] = colour
            out.append(jnp.sum(weight * colour, axis=0, keepdims=True))
        out.append(after_all[planes - 1 : planes])
        return out

    def share_of(r):
        return ray[r : r + 1, :].astype(jnp.float32) * 0.5

    def put(seg_out, r, values):
        for v in range(channels):
            for p in range(pieces):
                seg_out[p, v, r : r + 1, :] = values[v][:, p * piece : (p + 1) * piece]

    def when_reduces(who, work):
        if pieces < depths:
            pl.when(who < pieces)(work)
        else:
            work()

    def seg_copy(seg_out, seg_in, send, recv, d, source=None):
        to = lax.rem(k + d, depths)
        slot = k if source is None else source
        return pltpu.make_async_remote_copy(
            seg_out.at[to % pieces], seg_in.at[slot], send.at[d], recv.at[slot],
            device_id={"depth": to}, device_id_type=MESH,
        )

    def send_segments(seg_out, seg_in, send, recv):
        for d in range(1, depths):
            when_reduces(lax.rem(k + d, depths), seg_copy(seg_out, seg_in, send, recv, d).start)

        def own():
            seg_in[k] = seg_out[k % pieces]

        when_reduces(k, own)

    def reduce(seg_in, qd_out, send, recv, first, count):
        for d in range(1, depths):
            source = lax.rem(k + d, depths)
            seg_copy(seg_in, seg_in, send, recv, d, source).wait_recv()
        at = pl.ds(pl.multiple_of((k % pieces) * piece, piece), piece)
        fronts = [None]
        front = seg_in[0, 3]
        pixel = [seg_in[0, c] for c in range(3)]
        fronts.append(front)
        for j in range(1, depths):
            for c in range(3):
                pixel[c] = pixel[c] + front * seg_in[j, c]
            front = front * seg_in[j, 3]
            fronts.append(front)
        half = 0.5 * planes * depths
        pg = [half * (pixel[c] + front - tgt[c, first : first + count, at]) for c in range(3)]
        behind = pg[0] + pg[1] + pg[2]
        for j in range(depths - 1, -1, -1):
            for c in range(3):
                qd_out[j, c] = pg[c] if j == 0 else fronts[j] * pg[c]
            qd_out[j, 3] = fronts[j + 1] * behind
            if j:
                behind = pg[0] * seg_in[j, 0] + pg[1] * seg_in[j, 1] + pg[2] * seg_in[j, 2] + seg_in[j, 3] * behind

    def qd_copy(qd_out, qd_in, send, recv, d, source=None):
        to = lax.rem(k + d, depths)
        slot = k % pieces if source is None else source % pieces
        return pltpu.make_async_remote_copy(
            qd_out.at[to], qd_in.at[slot], send.at[d], recv.at[slot],
            device_id={"depth": to}, device_id_type=MESH,
        )

    def qd_copy_next(d, source=None):
        to = lax.rem(k + d, depths)
        slot = k % pieces if source is None else source % pieces
        return pltpu.make_async_remote_copy(
            qd2_out.at[to], qdp_in.at[slot], qp_send.at[d], qp_recv.at[slot],
            device_id={"tile": t + 1, "depth": to}, device_id_type=MESH,
        )

    def send_back(qd_out, qd_in, send, recv):
        for d in range(1, depths):
            qd_copy(qd_out, qd_in, send, recv, d).start()
        qd_in[k % pieces] = qd_out[k]

    def wait_back(qd_in, send, recv):
        for d in range(1, depths):
            source = lax.rem(k + d, depths)
            when_reduces(source, qd_copy(qd_in, qd_in, send, recv, d, source).wait_recv)

    lanes = lax.broadcasted_iota(jnp.int32, (planes, width), 1)

    def smooth_within(c):
        for r in range(rows):
            here = g[c, r]
            around = jnp.where(planes_at == 0, 0.0, pltpu.roll(here, 1, 0))
            around += jnp.where(planes_at == planes - 1, 0.0, pltpu.roll(here, planes - 1, 0))
            around += jnp.where(lanes == 0, 0.0, pltpu.roll(here, 1, 1))
            around += jnp.where(lanes == width - 1, 0.0, pltpu.roll(here, width - 1, 1))
            if r > 0:
                around += g[c, r - 1]
            if r < last:
                around += g[c, r + 1]
            grad_ref[c, r] = 2.0 * tv_weight * (6.0 * here - around)

    for r in range(last):
        values = samples(r, lambda c: g[c, r], lambda c: g[c, r + 1], share_of(r), occ)
        put(seg1_out, r, values)
    send_segments(seg1_out, seg1_in, s1_send, s1_recv)

    for c in range(channels // 2):
        smooth_within(c)

    @pl.when(has_next)
    def _():
        to_prev.wait_recv()
        to_next.start()
        ext_next.start()

    values = samples(last, lambda c: g[c, last], lambda c: nxt[c, 0], share_of(last), occ)
    put(seg2_out, 0, values)
    send_segments(seg2_out, seg2_in, s2_send, s2_recv)

    def first_rows():
        reduce(seg1_in, qd1_out, s1_send, s1_recv, 0, last)
        send_back(qd1_out, qd1_in, q1_send, q1_recv)

    for c in range(channels // 2, channels):
        smooth_within(c)

    def last_row():
        reduce(seg2_in, qd2_out, s2_send, s2_recv, last, 1)

        @pl.when(has_next)
        def _():
            for d in range(depths):
                qd_copy_next(d).start()

        send_back(qd2_out, qd2_in, q2_send, q2_recv)

    when_reduces(k, last_row)

    when_reduces(k, first_rows)

    pl.when(k > 0)(z_back.wait_recv)
    pl.when(k < depths - 1)(z_front.wait_recv)
    for c in range(channels):
        for r in range(rows):
            i = c * rows + r
            grad_ref[c, r, 0:1, :] -= 2.0 * tv_weight * zin[0, i : i + 1, :]
            grad_ref[c, r, planes - 1 : planes, :] -= 2.0 * tv_weight * zin[1, i : i + 1, :]
        grad_ref[c, last] -= 2.0 * tv_weight * nxt[c, 0]

    def gradient(slot, qd_in, r):
        q = [jnp.concatenate([qd_in[p, v, r : r + 1, :] for p in range(pieces)], axis=1) for v in range(4)]
        u = q[0] * col[slot, 0] + q[1] * col[slot, 1] + q[2] * col[slot, 2]
        weight = wgt[slot]
        part = weight * u
        rest = running_sum(part, planes_at, True) - part
        out = [(ntr[slot] * u - rest - q[3]) * dfac[slot]]
        for c in range(3):
            colour = col[slot, c]
            out.append(q[c] * weight * (colour * (1.0 - colour)))
        return out

    def add(r, factor, values):
        for c in range(channels):
            grad_ref[c, r] += factor * values[c]

    wait_back(qd1_in, q1_send, q1_recv)
    for r in range(last):
        values = gradient(r, qd1_in, r)
        add(r, 1.0 - share_of(r), values)
        add(r + 1, share_of(r), values)
    @pl.when(has_prev)
    def _():
        to_next.wait_recv()
        ext_next.wait_recv()

    samples(rows, lambda c: prv[c, 0], lambda c: g[c, 0], ext_in[0:1, :], ext_in[1:2, :])
    for c in range(channels):
        grad_ref[c, 0] -= 2.0 * tv_weight * prv[c, 0]

    wait_back(qd2_in, q2_send, q2_recv)
    add(last, 1.0 - share_of(last), gradient(last, qd2_in, 0))

    @pl.when(has_prev)
    def _():
        for d in range(depths):
            source = lax.rem(k + d, depths)
            when_reduces(source, qd_copy_next(d, source).wait_recv)

    add(0, ext_in[0:1, :], gradient(rows, qdp_in, 0))

    pl.when(has_prev)(to_prev.wait_send)

    @pl.when(has_next)
    def _():
        to_next.wait_send()
        ext_next.wait_send()

    pl.when(k < depths - 1)(z_back.wait_send)
    pl.when(k > 0)(z_front.wait_send)
    for d in range(1, depths):
        to = lax.rem(k + d, depths)
        when_reduces(to, seg_copy(seg1_out, seg1_in, s1_send, s1_recv, d).wait_send)
        when_reduces(to, seg_copy(seg2_out, seg2_in, s2_send, s2_recv, d).wait_send)

    def sent_back():
        for d in range(1, depths):
            qd_copy(qd1_out, qd1_in, q1_send, q1_recv, d).wait_send()
            qd_copy(qd2_out, qd2_in, q2_send, q2_recv, d).wait_send()

        @pl.when(has_next)
        def _():
            for d in range(depths):
                qd_copy_next(d).wait_send()

    when_reduces(k, sent_back)


def gradient_of_loss(grid, ray_offset, occupancy, target, tiles, depths):
    channels, rows, planes, width = grid.shape
    pieces = max(1, min(depths, width // 128))
    piece = width // pieces
    f32 = jnp.float32
    vmem, dma = pltpu.VMEM, pltpu.SemaphoreType.DMA
    scratch = [
        vmem(grid.shape, f32), vmem(ray_offset.shape, jnp.int32), vmem(occupancy.shape, jnp.int32),
        vmem(target.shape, f32),
        vmem((channels, 1, planes, width), f32), vmem((channels, 1, planes, width), f32),
        vmem((8, width), f32), vmem((8, width), f32),
        vmem((2, channels * rows, width), f32), vmem((2, channels * rows, width), f32),
        vmem((rows + 1, 3, planes, width), f32), vmem((rows + 1, planes, width), f32),
        vmem((rows + 1, planes, width), f32), vmem((rows + 1, planes, width), f32),
    ]
    for count in (rows - 1, 1):
        scratch += [vmem((pieces, 4, count, piece), f32), vmem((depths, 4, count, piece), f32)]
    for count in (rows - 1, 1):
        scratch += [vmem((depths, 4, count, piece), f32), vmem((pieces, 4, count, piece), f32)]
    scratch += [vmem((pieces, 4, 1, piece), f32)]
    scratch += [dma((4,)), dma((5,)), dma((5,))] + [dma((depths,))] * 10
    hbm = pl.BlockSpec(memory_space=pltpu.HBM)
    return pl.pallas_call(
        functools.partial(kernel, tiles, depths, pieces),
        out_shape=pltpu.VMEM(grid.shape, f32),
        in_specs=[hbm] * 4,
        out_specs=pl.BlockSpec(memory_space=pltpu.VMEM),
        scratch_shapes=scratch,
        compiler_params=pltpu.CompilerParams(
            collective_id=0, has_side_effects=True, vmem_limit_bytes=24 * 2**20
        ),
        cost_estimate=pl.CostEstimate(flops=10**7, bytes_accessed=2**20, transcendentals=10**6),
    )(*(pltpu.with_memory_space_constraint(x, pltpu.HBM) for x in (grid, ray_offset, occupancy, target)))


def solution(mesh):
    tiles, depths = mesh.shape["tile"], mesh.shape["depth"]
    voxels = P(None, "tile", "depth", None)
    in_specs = (voxels, voxels, voxels, P("tile", None), P("tile", "depth", None), P(None, "tile", None))

    def body(grid, first_moment, second_moment, ray_offset, occupancy, target):
        grad = gradient_of_loss(grid, ray_offset, occupancy, target, tiles, depths)
        new_first = beta_one * first_moment + (1.0 - beta_one) * grad
        new_second = beta_two * second_moment + (1.0 - beta_two) * grad * grad
        corr_one = 1.0 - beta_one**adam_step
        corr_two = 1.0 - beta_two**adam_step
        new_grid = grid - learn_rate * (new_first / corr_one) / (jnp.sqrt(new_second / corr_two) + epsilon)
        return (new_grid, new_first, new_second)

    return jax.shard_map(body, mesh=mesh, in_specs=in_specs, out_specs=(voxels,) * 3, check_vma=False)
```
